32 devices in a mesh: groups: 2 (over y), tiles: 4 (over z), chan: 2 (over x), sub: 2 (over core).
Axes of the slice: x: 2, y: 2, z: 4, core: 2. Of those that a mesh axis runs over, the one named last changes fastest.
Arguments:
- features: bfloat16 [128, 256, 256], P(('groups', 'tiles', 'sub'), 'chan'), parts along dimension 0, may hold values from -6 to 6
- cotangent: bfloat16 [128, 256, 256], P(('groups', 'tiles', 'sub'), 'chan'), parts along dimension 0, may hold values from -6 to 6
- down_factor: bfloat16 [2, 256, 64], P(None, 'chan'), may hold values from -0.375 to 0.375
- core_kernel: bfloat16 [2, 9, 64, 64], replicated, may hold values from -0.25 to 0.25
- up_factor: bfloat16 [2, 256, 64], P(None, 'chan'), may hold values from -0.75 to 0.75
- tile_count: int32 [16], P(('groups', 'tiles', 'sub')), parts along dimension 0, may hold values from 4 to 8, as said below
- neighbour_owner: int32 [128, 8], P(('groups', 'tiles', 'sub')), parts along dimension 0, may hold values from -1 to 7, as said below
- neighbour_slot: int32 [128, 8], P(('groups', 'tiles', 'sub')), parts along dimension 0, may hold values from -1 to 7, as said below
Outputs:
- input_gradient: bfloat16 [128, 256, 256], P(('groups', 'tiles', 'sub'), 'chan'), parts along dimension 0
- down_gradient: float32 [4, 256, 64], P('groups', 'chan'), parts along dimension 0
- core_gradient: float32 [4, 9, 64, 64], P('groups', None, 'chan'), parts along dimension 0
- up_gradient: float32 [4, 256, 64], P('groups', 'chan'), parts along dimension 0
The draws below stay inside these ranges and needn't reach their ends.
There are 2 independent parts, one for each index of `groups`. The reference program is written for one: setup_inputs(seed, part) draws one part's arguments, and reference() takes and returns one part's arrays. A program takes and returns all parts, laid end to end along the dimension named above; an argument that names none is the same for every part. Nothing has to cross between parts.
Inputs may be any that keep to these rules, and one draw needn't show every extreme that they name: `tile_count`: every count is even; some device holds exactly 8 live tiles and some exactly 4. `neighbour_owner`: -1 where the slot is not live or no tissue tile lies in that direction. Otherwise the owner is the slot's own device or the device just before or after it along the owners, and the named slot is live there. Neighbourhood is mutual: if tile h lies in some direction of tile g, then g lies in the opposite direction of h. `neighbour_slot`: -1 exactly where neighbour_owner is -1.
All inputs are finite; a program needn't handle non-finite values.
Results may differ from the reference program's by a relative error of at most 0.014.
Values may be sent and summed in bfloat16 or wider, within the bound.
A program may use at most 64 MiB of HBM per device.

```python
import jax
import jax.numpy as jnp
import numpy as np
from jax import lax

C = 256
RANK = 64
TILE = 16
SLOTS = 8
LAYERS = 2
OWNERS = 8
TILES_ALL = 64
GRID_W = 2
N_CHAN = 2


NEIGHBOUR_STEPS = np.array([[-1, -1], [-1, 0], [-1, 1], [0, -1], [0, 1], [1, -1], [1, 0], [1, 1]], np.int32)


def tissue_layout(key):
    layout_key = jax.random.fold_in(key, 7)
    key_pairs, key_full, key_small, key_gaps = jax.random.split(layout_key, 4)
    quarter = SLOTS // 4
    devices = jnp.arange(OWNERS)
    pair_count = jax.random.randint(key_pairs, (OWNERS,), quarter, 2 * quarter + 1)
    fullest = jax.random.randint(key_full, (), 0, OWNERS)
    emptiest = (fullest + 1 + jax.random.randint(key_small, (), 0, OWNERS - 1)) % OWNERS
    pair_count = jnp.where(devices == fullest, 2 * quarter, pair_count)
    pair_count = jnp.where(devices == emptiest, quarter, pair_count)
    counts = (2 * pair_count).astype(jnp.int32)
    run_ends = jnp.cumsum(counts).astype(jnp.int32)
    starts = run_ends - counts
    live_total = run_ends[-1]
    slot_total = OWNERS * SLOTS
    pair_gaps = jax.random.randint(key_gaps, (slot_total // 2,), 0, 2)
    pair_place = (jnp.arange(slot_total // 2) + jnp.cumsum(pair_gaps)).astype(jnp.int32)
    tile_ids = jnp.arange(slot_total).astype(jnp.int32)
    placement = pair_place[tile_ids // 2]
    half_width = GRID_W // 2
    tile_row = placement // half_width
    tile_col = 2 * (placement % half_width) + tile_ids % 2
    position = (tile_row * GRID_W + tile_col).astype(jnp.int32)
    slot_index = jnp.arange(SLOTS).astype(jnp.int32)
    slot_live = slot_index[None, :] < counts[:, None]
    slot_tile = jnp.where(slot_live, starts[:, None] + slot_index[None, :], 0).reshape(-1)
    slot_live = slot_live.reshape(-1)
    target_row = tile_row[slot_tile][:, None] + NEIGHBOUR_STEPS[None, :, 0]
    target_col = tile_col[slot_tile][:, None] + NEIGHBOUR_STEPS[None, :, 1]
    target = (target_row * GRID_W + target_col).astype(jnp.int32)
    inside = (target_col >= 0) & (target_col < GRID_W) & (target_row >= 0)
    found_at = jnp.searchsorted(position, target).astype(jnp.int32)
    found_clip = jnp.minimum(found_at, slot_total - 1)
    linked = inside & (position[found_clip] == target) & (found_at < live_total) & slot_live[:, None]
    owner_found = jnp.minimum(jnp.searchsorted(run_ends, found_clip, side='right'), OWNERS - 1).astype(jnp.int32)
    slot_found = found_clip - starts[owner_found]
    owner_found = jnp.where(linked, owner_found, -1).astype(jnp.int32)
    slot_found = jnp.where(linked, slot_found, -1).astype(jnp.int32)
    return (counts, owner_found, slot_found)


def draw_tile_count(key, part):
    return tissue_layout(key)[0]


def draw_neighbour_owner(key, part):
    return tissue_layout(key)[1]


def draw_neighbour_slot(key, part):
    return tissue_layout(key)[2]


def steps_of(stream_key, dims, pieces, least, high):
    level, own = 1.0, jax.random.fold_in(stream_key, 6)
    for axis_at, parts in pieces:
        heights = jnp.exp(jax.random.uniform(jax.random.fold_in(own, axis_at), (parts,), jnp.float32, least / len(pieces), high / len(pieces)))
        level = level * jnp.repeat(heights, dims[axis_at] // parts).reshape([-1 if axis == axis_at else 1 for axis in range(len(dims))])
    return level


def centred(own_key, extent, scale, most, cuts=(), kind=jnp.bfloat16):
    result = jax.random.normal(own_key, extent, jnp.float32) * scale
    if len(cuts) > 0:
        result = steps_of(own_key, extent, cuts, -0.22, 0.18) * result
    return jnp.clip(result, min=-most, max=most).astype(kind)


def setup_inputs(seed: int = 0, part: int = 0) -> dict:
    streams_of = jax.random.split(jax.random.key(seed), 9)
    own_keys = jax.random.split(jax.random.fold_in(streams_of[8], part), 9)
    return {
        "features": centred(own_keys[0], (TILES_ALL, C, TILE * TILE), 1.0, 6.0, ((0, 8), (1, 2))),
        "cotangent": centred(own_keys[1], (TILES_ALL, C, TILE * TILE), 1.0, 6.0, ((0, 8), (1, 2))),
        "down_factor": centred(streams_of[2], (LAYERS, C, RANK), C ** -0.5, 0.375, ((1, 2),)),
        "core_kernel": centred(streams_of[3], (LAYERS, 9, RANK, RANK), (9 * RANK) ** -0.5, 0.25),
        "up_factor": centred(streams_of[4], (LAYERS, C, RANK), RANK ** -0.5, 0.75, ((1, 2),)),
        "tile_count": draw_tile_count(jax.random.fold_in(jax.random.fold_in(streams_of[8], part), 71), part),
        "neighbour_owner": draw_neighbour_owner(jax.random.fold_in(jax.random.fold_in(streams_of[8], part), 71), part),
        "neighbour_slot": draw_neighbour_slot(jax.random.fold_in(jax.random.fold_in(streams_of[8], part), 71), part),
    }


EDGE_ROWS = [1, 6, 3, 4]
EDGE_PIECES = [1, 0, 3, 2]
CORNER_ROWS = [0, 2, 5, 7]
CORNER_PIECES = [3, 2, 1, 0]


def cycle_of(squares):
    edge_cells = jnp.concatenate([squares[:, :, 0, :], squares[:, :, -1, :], squares[:, :, :, 0], squares[:, :, :, -1]], axis=2)
    corners = jnp.stack([squares[:, :, 0, 0], squares[:, :, 0, -1], squares[:, :, -1, 0], squares[:, :, -1, -1]], axis=2)
    return jnp.concatenate([edge_cells, corners], axis=2)


def assemble(squares, side_cells, corner_cells):
    top_row = jnp.concatenate([corner_cells[0][:, :, None], side_cells[0], corner_cells[1][:, :, None]], axis=2)
    bottom_row = jnp.concatenate([corner_cells[2][:, :, None], side_cells[1], corner_cells[3][:, :, None]], axis=2)
    middle = jnp.concatenate([side_cells[2][:, :, :, None], squares, side_cells[3][:, :, :, None]], axis=3)
    return jnp.concatenate([top_row[:, :, None, :], middle, bottom_row[:, :, None, :]], axis=2)


def pad_all(flat_cells, neighbour_owner, neighbour_slot):
    squares = flat_cells.reshape(flat_cells.shape[0], flat_cells.shape[1], TILE, TILE)
    border = cycle_of(squares)
    present = neighbour_owner >= 0
    source = jnp.where(present, neighbour_owner * SLOTS + neighbour_slot, 0).astype(jnp.int32)
    weights = present.astype(flat_cells.dtype)
    side_cells = []
    for direction, piece_index in zip(EDGE_ROWS, EDGE_PIECES):
        picked = jnp.take(border, source[:, direction], axis=0)[:, :, piece_index * TILE:(piece_index + 1) * TILE]
        side_cells.append(picked * weights[:, direction, None, None])
    corner_cells = []
    for direction, piece_index in zip(CORNER_ROWS, CORNER_PIECES):
        picked = jnp.take(border, source[:, direction], axis=0)[:, :, 4 * TILE + piece_index]
        corner_cells.append(picked * weights[:, direction, None])
    return assemble(squares, side_cells, corner_cells)


def window(padded, shift_rows, shift_cols):
    section = padded[:, :, shift_rows:shift_rows + TILE, shift_cols:shift_cols + TILE]
    return section.reshape(section.shape[0], section.shape[1], TILE * TILE)


def forward_conv(padded, kernel):
    running = jnp.zeros((padded.shape[0], kernel.shape[1], TILE * TILE), jnp.float32)
    for offset in range(9):
        running = running + jnp.einsum("sr,urq->usq", kernel[offset].astype(jnp.float32), window(padded, offset // 3, offset % 3).astype(jnp.float32))
    return running


def backward_conv(padded, kernel):
    running = jnp.zeros((padded.shape[0], kernel.shape[2], TILE * TILE), jnp.float32)
    for offset in range(9):
        running = running + jnp.einsum("sr,usq->urq", kernel[offset].astype(jnp.float32), window(padded, 2 - offset // 3, 2 - offset % 3).astype(jnp.float32))
    return running


def core_gradient_of(gradient, padded):
    taps = [jnp.einsum("usq,urq->sr", gradient.astype(jnp.float32), window(padded, offset // 3, offset % 3).astype(jnp.float32)) for offset in range(9)]
    return jnp.stack(taps, axis=0)


def blocked_sum(factor, data):
    width = C // N_CHAN
    running = jnp.zeros((data.shape[0], factor.shape[1], data.shape[2]), jnp.float32)
    for member in range(N_CHAN):
        partial_value = jnp.einsum("cr,ucq->urq", factor[member * width:(member + 1) * width].astype(jnp.float32), data[:, member * width:(member + 1) * width].astype(jnp.float32))
        running = running + lax.optimization_barrier(partial_value.astype(jnp.bfloat16)).astype(jnp.float32)
    return running.astype(jnp.bfloat16)


def reference(features, cotangent, down_factor, core_kernel, up_factor, tile_count, neighbour_owner, neighbour_slot):
    slot_ids = jnp.arange(TILES_ALL).astype(jnp.int32)
    owner_of = (slot_ids // SLOTS).astype(jnp.int32)
    alive = ((slot_ids % SLOTS) < tile_count[owner_of]).astype(jnp.bfloat16)
    hidden = features * alive[:, None, None]
    upstream = cotangent * alive[:, None, None]
    saved_layers = []
    for layer_index in range(LAYERS):
        activations = blocked_sum(down_factor[layer_index], hidden)
        padded = pad_all(activations, neighbour_owner, neighbour_slot)
        mixed = forward_conv(padded, core_kernel[layer_index]).astype(jnp.bfloat16)
        preact = jnp.einsum("cs,usq->ucq", up_factor[layer_index].astype(jnp.float32), mixed.astype(jnp.float32))
        saved_layers.append((hidden, padded, mixed, preact))
        hidden = (hidden.astype(jnp.float32) + jax.nn.silu(preact)).astype(jnp.bfloat16)
    down_list = [None] * LAYERS
    core_list = [None] * LAYERS
    up_list = [None] * LAYERS
    for layer_index in reversed(range(LAYERS)):
        hidden, padded, mixed, preact = saved_layers[layer_index]
        squashed = jax.nn.sigmoid(preact)
        pre_gradient = (upstream.astype(jnp.float32) * squashed * (1.0 + preact * (1.0 - squashed))).astype(jnp.bfloat16)
        up_list[layer_index] = jnp.einsum("ucq,usq->cs", pre_gradient.astype(jnp.float32), mixed.astype(jnp.float32))
        mixed_gradient = blocked_sum(up_factor[layer_index], pre_gradient)
        core_list[layer_index] = core_gradient_of(mixed_gradient, padded)
        gradient_padded = pad_all(mixed_gradient, neighbour_owner, neighbour_slot)
        act_gradient = backward_conv(gradient_padded, core_kernel[layer_index]).astype(jnp.bfloat16)
        down_list[layer_index] = jnp.einsum("ucq,urq->cr", hidden.astype(jnp.float32), act_gradient.astype(jnp.float32))
        through = jnp.einsum("cr,urq->ucq", down_factor[layer_index].astype(jnp.float32), act_gradient.astype(jnp.float32))
        upstream = (upstream.astype(jnp.float32) + through).astype(jnp.bfloat16)
    return upstream, jnp.stack(down_list, axis=0), jnp.stack(core_list, axis=0), jnp.stack(up_list, axis=0)
```

```python
import jax
import jax.numpy as jnp
from jax import lax
from jax.sharding import PartitionSpec as P

TILE = 16
LAYERS = 2


EDGE_ROWS = [1, 6, 3, 4]
EDGE_PIECES = [1, 0, 3, 2]
CORNER_ROWS = [0, 2, 5, 7]
CORNER_PIECES = [3, 2, 1, 0]


def padded_2(cells, sides, width):
    for axis, dim in sides:
        count = lax.axis_size(axis)
        ends = count - 1
        head = lax.slice_in_dim(cells, 0, width, axis=dim)
        tail = lax.slice_in_dim(cells, cells.shape[dim] - width, cells.shape[dim], axis=dim)
        cells = jnp.concatenate(
            [
                lax.ppermute(tail, axis, [(i, (i + 1) % count) for i in range(ends)]),
                cells,
                lax.ppermute(head, axis, [((i + 1) % count, i) for i in range(ends)]),
            ],
            axis=dim,
        )
    return cells


def cycle_of(squares):
    edge_cells = jnp.concatenate(
        [squares[:, :, 0, :], squares[:, :, -1, :], squares[:, :, :, 0], squares[:, :, :, -1]],
        axis=2,
    )
    corners = jnp.stack(
        [squares[:, :, 0, 0], squares[:, :, 0, -1], squares[:, :, -1, 0], squares[:, :, -1, -1]],
        axis=2,
    )
    return jnp.concatenate([edge_cells, corners], axis=2)


def assemble(squares, side_cells, corner_cells):
    top_row = jnp.concatenate(
        [corner_cells[0][:, :, None], side_cells[0], corner_cells[1][:, :, None]], axis=2
    )
    bottom_row = jnp.concatenate(
        [corner_cells[2][:, :, None], side_cells[1], corner_cells[3][:, :, None]], axis=2
    )
    middle = jnp.concatenate(
        [side_cells[2][:, :, :, None], squares, side_cells[3][:, :, :, None]], axis=3
    )
    return jnp.concatenate([top_row[:, :, None, :], middle, bottom_row[:, :, None, :]], axis=2)


def selectors(neighbour_owner, neighbour_slot, device_here, slot_total):
    local_row = (neighbour_owner - device_here + 1) * slot_total + neighbour_slot
    columns = jnp.arange(3 * slot_total)
    matched = (local_row[:, :, None] == columns[None, None, :]) & (neighbour_owner[:, :, None] >= 0)
    return matched.astype(jnp.bfloat16)


def place_border(flat_cells, extended, chooser):
    squares = flat_cells.reshape(flat_cells.shape[0], flat_cells.shape[1], TILE, TILE)
    nearest = jnp.einsum(
        "uvd,dck->uvck",
        jnp.stack([chooser[:, row] for row in EDGE_ROWS], axis=1),
        extended[:, :, : 4 * TILE],
        preferred_element_type=jnp.float32,
    ).astype(jnp.bfloat16)
    diagonal = jnp.einsum(
        "uvd,dck->uvck",
        jnp.stack([chooser[:, row] for row in CORNER_ROWS], axis=1),
        extended[:, :, 4 * TILE :],
        preferred_element_type=jnp.float32,
    ).astype(jnp.bfloat16)
    side_cells = [
        nearest[:, which_side, :, piece_index * TILE : (piece_index + 1) * TILE]
        for which_side, piece_index in enumerate(EDGE_PIECES)
    ]
    corner_cells = [
        diagonal[:, which_side, :, piece_index]
        for which_side, piece_index in enumerate(CORNER_PIECES)
    ]
    return assemble(squares, side_cells, corner_cells)


def window(padded, shift_rows, shift_cols):
    section = padded[:, :, shift_rows : shift_rows + TILE, shift_cols : shift_cols + TILE]
    return section.reshape(section.shape[0], section.shape[1], TILE * TILE)


def stacked_windows(padded, flipped):
    if flipped:
        return jnp.stack(
            [window(padded, 2 - offset // 3, 2 - offset % 3) for offset in range(9)], axis=0
        )
    return jnp.stack([window(padded, offset // 3, offset % 3) for offset in range(9)], axis=0)


def forward_conv(windows, kernel):
    return jnp.einsum("tsr,turq->usq", kernel, windows, preferred_element_type=jnp.float32)


def backward_conv(padded, kernel):
    return jnp.einsum(
        "tsr,tusq->urq", kernel, stacked_windows(padded, True), preferred_element_type=jnp.float32
    )


def core_gradient_of(gradient, windows):
    return jnp.einsum("usq,turq->tsr", gradient, windows, preferred_element_type=jnp.float32)


def blocked_product(factor, data, members):
    width = factor.shape[0] // members
    running = jnp.zeros((data.shape[0], factor.shape[1], data.shape[2]), jnp.float32)
    for member in range(members):
        partial_value = jnp.einsum(
            "cr,ucq->urq",
            factor[member * width : (member + 1) * width],
            data[:, member * width : (member + 1) * width],
            preferred_element_type=jnp.float32,
        )
        running = running + lax.optimization_barrier(partial_value.astype(jnp.bfloat16)).astype(
            jnp.float32
        )
    return running.astype(jnp.bfloat16)


def settle(down_part, core_part, up_part):
    return (down_part, core_part, up_part)


def whole_tiles(
    features,
    cotangent,
    down_factor,
    core_kernel,
    up_factor,
    tile_count,
    neighbour_owner,
    neighbour_slot,
):
    slot_total = features.shape[0]
    members = lax.axis_size("chan")
    rows_here = slot_total // members
    device_here = lax.axis_index(("tiles", "sub"))
    first_slot = lax.axis_index("chan") * rows_here
    hidden, upstream = (
        lax.all_to_all(features, "chan", split_axis=0, concat_axis=1, tiled=True),
        lax.all_to_all(cotangent, "chan", split_axis=0, concat_axis=1, tiled=True),
    )
    alive = (first_slot + jnp.arange(rows_here) < tile_count[0]).astype(jnp.bfloat16)
    hidden = hidden * alive[:, None, None]
    upstream = upstream * alive[:, None, None]
    down_whole, up_whole = (
        lax.all_gather(down_factor, "chan", axis=1, tiled=True),
        lax.all_gather(up_factor, "chan", axis=1, tiled=True),
    )
    near_owner = lax.dynamic_slice_in_dim(neighbour_owner, first_slot, rows_here, 0)
    near_slot = lax.dynamic_slice_in_dim(neighbour_slot, first_slot, rows_here, 0)
    chooser = selectors(near_owner, near_slot, device_here, slot_total)

    def padded_of(cells):
        border = cycle_of(cells.reshape(rows_here, cells.shape[1], TILE, TILE))
        owner_cycle = lax.all_gather(border, "chan", axis=0, tiled=True)
        extended = padded_2(owner_cycle, ((("tiles", "sub"), 0),), slot_total)
        return place_border(cells, extended, chooser)

    saved_layers = []
    for layer_index in range(LAYERS):
        activations = blocked_product(down_whole[layer_index], hidden, members)
        windows = stacked_windows(padded_of(activations), False)
        mixed = forward_conv(windows, core_kernel[layer_index]).astype(jnp.bfloat16)
        preact = jnp.einsum(
            "cs,usq->ucq", up_whole[layer_index], mixed, preferred_element_type=jnp.float32
        )
        saved_layers.append((hidden, windows, mixed, preact))
        hidden = (hidden.astype(jnp.float32) + jax.nn.silu(preact)).astype(jnp.bfloat16)
    down_list = [None] * LAYERS
    core_list = [None] * LAYERS
    up_list = [None] * LAYERS
    for layer_index in reversed(range(LAYERS)):
        hidden, windows, mixed, preact = saved_layers[layer_index]
        squashed = jax.nn.sigmoid(preact)
        pre_gradient = (
            upstream.astype(jnp.float32) * squashed * (1.0 + preact * (1.0 - squashed))
        ).astype(jnp.bfloat16)
        up_part = jnp.einsum("ucq,usq->cs", pre_gradient, mixed, preferred_element_type=jnp.float32)
        mixed_gradient = blocked_product(up_whole[layer_index], pre_gradient, members)
        core_part = core_gradient_of(mixed_gradient, windows)
        gradient_padded = padded_of(mixed_gradient)
        act_gradient = backward_conv(gradient_padded, core_kernel[layer_index]).astype(jnp.bfloat16)
        down_part = jnp.einsum(
            "ucq,urq->cr", hidden, act_gradient, preferred_element_type=jnp.float32
        )
        through = jnp.einsum(
            "cr,urq->ucq", down_whole[layer_index], act_gradient, preferred_element_type=jnp.float32
        )
        upstream = (upstream.astype(jnp.float32) + through).astype(jnp.bfloat16)
        down_part, up_part = (
            lax.psum_scatter(
                down_part.astype(jnp.bfloat16), "chan", scatter_dimension=0, tiled=True
            ).astype(jnp.float32),
            lax.psum_scatter(
                up_part.astype(jnp.bfloat16), "chan", scatter_dimension=0, tiled=True
            ).astype(jnp.float32),
        )
        core_part = lax.psum_scatter(
            core_part.astype(jnp.bfloat16), "chan", scatter_dimension=1, tiled=True
        ).astype(jnp.float32)
        down_list[layer_index], core_list[layer_index], up_list[layer_index] = settle(
            down_part, core_part, up_part
        )
    upstream = lax.all_to_all(upstream, "chan", split_axis=1, concat_axis=0, tiled=True)
    return (upstream, down_list, core_list, up_list)


def local(
    features,
    cotangent,
    down_factor,
    core_kernel,
    up_factor,
    tile_count,
    neighbour_owner,
    neighbour_slot,
):
    upstream, down_list, core_list, up_list = whole_tiles(
        features,
        cotangent,
        down_factor,
        core_kernel,
        up_factor,
        tile_count,
        neighbour_owner,
        neighbour_slot,
    )
    down_gradient = jnp.stack(down_list, axis=0)
    core_gradient = jnp.stack(core_list, axis=0)
    up_gradient = jnp.stack(up_list, axis=0)
    down_gradient, core_gradient, up_gradient = lax.psum(
        (down_gradient, core_gradient, up_gradient), ("tiles", "sub")
    )
    return (upstream, down_gradient, core_gradient, up_gradient)


def solution(mesh):
    return jax.shard_map(
        local,
        mesh=mesh,
        in_specs=(
            P(("groups", "tiles", "sub"), "chan", None),
            P(("groups", "tiles", "sub"), "chan", None),
            P(None, "chan", None),
            P(),
            P(None, "chan", None),
            P(("groups", "tiles", "sub")),
            P(("groups", "tiles", "sub"), None),
            P(("groups", "tiles", "sub"), None),
        ),
        out_specs=(
            P(("groups", "tiles", "sub"), "chan", None),
            P("groups", "chan", None),
            P("groups", None, "chan", None),
            P("groups", "chan", None),
        ),
        check_vma=False,
    )
```

```python
import functools

import jax
import jax.numpy as jnp
import numpy as np
from jax import lax
from jax.experimental import pallas as pl
from jax.experimental.pallas import tpu as pltpu
from jax.sharding import PartitionSpec as P

TILE = 16
PIX = TILE * TILE
LAYERS = 2
HALO = 128
LANE_DIRECTIONS = [(6, 16), (1, 16), (4, 16), (3, 16), (7, 1), (5, 1), (2, 1), (0, 1)]
F32, BF16 = jnp.float32, jnp.bfloat16
MESH = pl.DeviceIdType.MESH


def border_matrix():
    chosen = np.zeros((PIX, HALO), np.float32)
    last = TILE - 1
    for k in range(TILE):
        chosen[k, k] = 1
        chosen[last * TILE + k, TILE + k] = 1
        chosen[k * TILE, 2 * TILE + k] = 1
        chosen[k * TILE + last, 3 * TILE + k] = 1
    for lane, pixel in enumerate((0, last, last * TILE, PIX - 1)):
        chosen[pixel, 4 * TILE + lane] = 1
    return chosen


def window_matrix():
    chosen = np.zeros((PIX + HALO, 9, TILE, TILE), np.float32)
    end = TILE + 1
    for tap in range(9):
        for i in range(TILE):
            for j in range(TILE):
                row, col = i + tap // 3, j + tap % 3
                if 0 < row < end and 0 < col < end:
                    source = (row - 1) * TILE + col - 1
                elif 0 < col < end:
                    source = PIX + (TILE if row == 0 else 0) + col - 1
                elif 0 < row < end:
                    source = PIX + (3 * TILE if col == 0 else 2 * TILE) + row - 1
                else:
                    source = PIX + 4 * TILE + (2 if row == 0 else 0) + (1 if col == 0 else 0)
                chosen[source, tap, i, j] = 1
    return chosen.reshape(PIX + HALO, 9 * PIX)


def nn(a, b):
    return jnp.dot(a, b, preferred_element_type=F32)


def nt(a, b):
    return lax.dot_general(a, b, (((1,), (1,)), ((), ())), preferred_element_type=F32)


def tn(a, b):
    return lax.dot_general(a, b, (((0,), (0,)), ((), ())), preferred_element_type=F32)


def kernel(
    sizes, feat, cot, down, up, kf, kb, alive, chooser, bsel, wsel,
    out, dgrad, ugrad, cgrad,
    inbox, fact, hid, grad_e, zs, bs, wins, mwin, border, ext, stage, outbox, gsend, grecv, csend, crecv, cown,
    send_sem, recv_sem, bsend_sem, brecv_sem,
):
    tiles, subs, members, here = sizes
    chan = lax.axis_index("chan")
    owner = lax.axis_index("tiles") * subs + lax.axis_index("sub")
    owners = tiles * subs
    has_prev, has_next = owner > 0, owner < owners - 1
    rank = down.shape[2]
    part = rank // members

    def peer(j):
        return (chan + j) % members

    def at(shift, c):
        o = owner + shift
        return {"tiles": o // subs, "sub": o % subs, "chan": c}

    near = [
        (shift, j, cond)
        for shift, cond in ((0, None), (1, has_next), (-1, has_prev))
        for j in range(members)
        if shift or j
    ]

    def guarded(cond, action):
        if cond is None:
            action()
        else:
            pl.when(cond)(action)

    @pl.when(jnp.logical_not(has_prev))
    def _():
        ext[:, 0] = jnp.zeros_like(ext[:, 0])

    @pl.when(jnp.logical_not(has_next))
    def _():
        ext[:, 2] = jnp.zeros_like(ext[:, 2])

    barrier = pltpu.get_barrier_semaphore()
    for shift, j, cond in near:
        def greet(shift=shift, j=j):
            pl.semaphore_signal(barrier, inc=1, device_id=at(shift, peer(j)), device_id_type=MESH)
        guarded(cond, greet)
    sides = has_prev.astype(jnp.int32) + has_next.astype(jnp.int32)
    pl.semaphore_wait(barrier, members - 1 + members * sides)

    def to_peer(k, j, src, dst):
        return pltpu.make_async_remote_copy(
            src_ref=src, dst_ref=dst, send_sem=send_sem.at[k, j], recv_sem=recv_sem.at[k, members - j],
            device_id={"chan": peer(j)}, device_id_type=MESH,
        )

    def from_peer(k, j, src, dst):
        return pltpu.make_async_remote_copy(
            src_ref=src, dst_ref=dst, send_sem=send_sem.at[k, j], recv_sem=recv_sem.at[k, j],
            device_id={"chan": peer(j)}, device_id_type=MESH,
        )

    def slots_of(j):
        return pl.ds(peer(j) * here, here)

    peers = range(1, members)
    sent, arrivals = [], {}

    def exchange(k, source, target):
        for j in peers:
            sent.append(to_peer(k, j, source(j), target.at[members - j]))
            sent[-1].start()
        arrivals[k] = [from_peer(k, j, source(j), target.at[j]) for j in peers]

    def arrived(k):
        for copy in arrivals[k]:
            copy.wait_recv()

    exchange(0, lambda j: down, fact.at[0])
    exchange(1, lambda j: feat.at[slots_of(j)], inbox.at[0])
    exchange(2, lambda j: up, fact.at[1])
    exchange(3, lambda j: cot.at[slots_of(j)], inbox.at[1])

    def lanes(x):
        return jnp.concatenate([x[u] for u in range(here)], axis=1)

    def live(x):
        return (lanes(x).astype(F32) * alive[...]).astype(BF16)

    hid[0, 0] = live(feat[slots_of(0)])
    grad_e[0] = live(cot[slots_of(0)])

    def field(factors, blocks):
        total = None
        for factor, block in zip(factors, blocks):
            part = tn(factor, block).astype(BF16).astype(F32)
            total = part if total is None else total + part
        return total.astype(BF16)

    def place(shift, j):
        return shift % 3 * members + j

    def border_copy(r, k):
        shift, j, cond = near[k]
        mirrored = place(-shift, (members - j) % members)
        return cond, pltpu.make_async_remote_copy(
            src_ref=border.at[r], dst_ref=ext.at[r, 1 - shift, chan],
            send_sem=bsend_sem.at[r, place(shift, j)], recv_sem=brecv_sem.at[r, mirrored],
            device_id=at(shift, peer(j)), device_id_type=MESH,
        )

    def border_arrival(r, k):
        shift, j, cond = near[k]
        return cond, pltpu.make_async_remote_copy(
            src_ref=border.at[r], dst_ref=ext.at[r, 1 + shift, peer(j)],
            send_sem=bsend_sem.at[r, place(shift, j)], recv_sem=brecv_sem.at[r, place(shift, j)],
            device_id=at(shift, peer(j)), device_id_type=MESH,
        )

    def send_border(r, rows):
        edge = nn(rows, bsel[...]).astype(BF16).reshape(here, rank, HALO)
        border[r] = edge
        for k in range(len(near)):
            cond, copy = border_copy(r, k)
            guarded(cond, copy.start)
        ext[r, 1, pl.ds(chan, 1)] = edge[None]

    def finish_border(r):
        for k in range(len(near)):
            cond, copy = border_arrival(r, k)
            guarded(cond, copy.wait_recv)

    def drain_border(r):
        for k in range(len(near)):
            cond, copy = border_copy(r, k)
            guarded(cond, copy.wait_send)

    def rows_of(value):
        return jnp.concatenate([value[:, u * PIX:(u + 1) * PIX] for u in range(here)], axis=0)

    def windows(r, rows, target):
        halos = [jnp.zeros((rank, HALO), F32) for _ in range(here)]
        for v in range(3 * members * here):
            piece = ext[r, v // (members * here), v // here % members, v % here].astype(F32)
            for u in range(here):
                w = u * 3 * members * here + v
                halos[u] = halos[u] + piece * chooser[w:w + 1, :]
        halo = jnp.concatenate(halos, axis=0).astype(BF16)
        both = jnp.concatenate([rows, halo], axis=1)
        for tap in range(9):
            moved = nn(both, wsel[:, tap * PIX:(tap + 1) * PIX]).astype(BF16)
            for u in range(here):
                target[tap * rank:(tap + 1) * rank, u * PIX:(u + 1) * PIX] = moved[u * rank:(u + 1) * rank]

    def factors(which, layer):
        own = (down, up)[which]
        return [own[layer]] + [fact[which, j, layer] for j in peers]

    arrived(0)
    arrived(1)
    for j in peers:
        hid[0, j] = live(inbox[0, j])
    for layer in range(LAYERS):
        act = field(factors(0, layer), [hid[layer, j] for j in range(members)])
        rows = rows_of(act)
        send_border(layer, rows)
        finish_border(layer)
        windows(layer, rows, wins.at[layer])
        b = nn(kf[layer], wins[layer]).astype(BF16)
        bs[layer] = b
        if layer == 0:
            arrived(2)
            arrived(3)
            for j in peers:
                grad_e[j] = live(inbox[1, j])
        for j, factor in enumerate(factors(1, layer)):
            z = nn(factor, b)
            zs[layer, j] = z
            if layer < LAYERS - 1:
                silu = z * jax.nn.sigmoid(z)
                hid[layer + 1, j] = (hid[layer, j].astype(F32) + silu).astype(BF16)
    for layer in reversed(range(LAYERS)):
        r = LAYERS + layer
        deltas = []
        for j in range(members):
            z = zs[layer, j]
            sig = jax.nn.sigmoid(z)
            e = grad_e[j].astype(F32)
            deltas.append((e * sig * (1.0 + z * (1.0 - sig))).astype(BF16))
        m = field(factors(1, layer), deltas)
        rows = rows_of(m)
        send_border(r, rows)
        core = nt(m, wins[layer])
        for c in range(members):
            piece = core[c * part:(c + 1) * part]
            cown[layer, c] = piece
            csend[layer, c] = piece.astype(BF16)
        exchange(5 + 3 * layer, lambda j: csend.at[layer, peer(j)], crecv.at[layer])
        ugrad[layer] = nt(deltas[0], bs[layer])
        for j in peers:
            gsend[layer, 1, j] = nt(deltas[j], bs[layer]).astype(BF16)
        exchange(6 + 3 * layer, lambda j: gsend.at[layer, 1, j], grecv.at[layer, 1])
        finish_border(r)
        windows(r, rows, mwin)
        n = nn(kb[layer], mwin[...]).astype(BF16)
        through_factors = factors(0, layer)
        for j in (*peers, 0):
            new_e = (grad_e[j].astype(F32) + nn(through_factors[j], n)).astype(BF16)
            if layer > 0:
                grad_e[j] = new_e
                continue
            for u in range(here):
                tile = new_e[:, u * PIX:(u + 1) * PIX]
                if j:
                    stage[j, u] = tile
                else:
                    out[pl.ds(chan * here + u, 1)] = tile[None]
            if j == members - 1:
                exchange(4, lambda i: stage.at[i], outbox)
        for j in peers:
            gsend[layer, 0, j] = nt(hid[layer, j], n).astype(BF16)
        exchange(7 + 3 * layer, lambda j: gsend.at[layer, 0, j], grecv.at[layer, 0])
        dgrad[layer] = nt(hid[layer, 0], n)
    for layer in reversed(range(LAYERS)):
        for k in range(3):
            arrived(5 + 3 * layer + k)
        total = cown[layer, pl.ds(chan, 1)][0]
        for j in peers:
            dgrad[layer] = dgrad[layer] + grecv[layer, 0, j].astype(F32)
            ugrad[layer] = ugrad[layer] + grecv[layer, 1, j].astype(F32)
            total = total + crecv[layer, j].astype(F32)
        cgrad[layer] = total
    arrived(4)
    for j in peers:
        for u in range(here):
            out[pl.ds(peer(j) * here + u, 1)] = outbox[j, u][None]
    for copy in sent:
        copy.wait_send()
    for r in range(2 * LAYERS):
        drain_border(r)


def local(sizes, features, cotangent, down_factor, core_kernel, up_factor, tile_count, neighbour_owner, neighbour_slot):
    tiles, subs, members = sizes
    slots, width, _ = features.shape
    here = slots // members
    rank = down_factor.shape[2]
    device = lax.axis_index(("tiles", "sub"))
    first = lax.axis_index("chan") * here
    owner = lax.dynamic_slice_in_dim(neighbour_owner, first, here, 0)
    slot = lax.dynamic_slice_in_dim(neighbour_slot, first, here, 0)
    row = jnp.where(owner >= 0, (owner - device + 1) * slots + slot, -1)
    lane_row = jnp.concatenate(
        [jnp.broadcast_to(row[:, d:d + 1], (here, n)) for d, n in LANE_DIRECTIONS]
        + [jnp.full((here, HALO - 4 * TILE - 4), -1, jnp.int32)],
        axis=1,
    )
    chooser = (lane_row[:, None, :] == jnp.arange(3 * slots)[None, :, None]).astype(F32).reshape(here * 3 * slots, HALO)
    alive = (first + jnp.arange(here * PIX) // PIX < tile_count[0]).astype(F32)[None]
    kf = core_kernel.transpose(0, 2, 1, 3).reshape(LAYERS, rank, 9 * rank)
    kb = core_kernel[:, ::-1].transpose(0, 3, 1, 2).reshape(LAYERS, rank, 9 * rank)
    pixels = here * PIX
    vmem = pl.BlockSpec(memory_space=pltpu.VMEM)
    dma = pltpu.SemaphoreType.DMA
    out, dgrad, ugrad, cgrad = pl.pallas_call(
        functools.partial(kernel, (tiles, subs, members, here)),
        out_shape=(
            jax.ShapeDtypeStruct(features.shape, BF16),
            jax.ShapeDtypeStruct((LAYERS, width, rank), F32),
            jax.ShapeDtypeStruct((LAYERS, width, rank), F32),
            jax.ShapeDtypeStruct((LAYERS, rank // members, 9 * rank), F32),
        ),
        in_specs=[vmem] * 10,
        out_specs=(vmem,) * 4,
        scratch_shapes=[
            pltpu.VMEM((2, members, here, width, PIX), BF16),
            pltpu.VMEM((2, members, LAYERS, width, rank), BF16),
            pltpu.VMEM((LAYERS, members, width, pixels), BF16),
            pltpu.VMEM((members, width, pixels), BF16),
            pltpu.VMEM((LAYERS, members, width, pixels), F32),
            pltpu.VMEM((LAYERS, rank, pixels), BF16),
            pltpu.VMEM((LAYERS, 9 * rank, pixels), BF16),
            pltpu.VMEM((9 * rank, pixels), BF16),
            pltpu.VMEM((2 * LAYERS, here, rank, HALO), BF16),
            pltpu.VMEM((2 * LAYERS, 3, members, here, rank, HALO), BF16),
            pltpu.VMEM((members, here, width, PIX), BF16),
            pltpu.VMEM((members, here, width, PIX), BF16),
            pltpu.VMEM((LAYERS, 2, members, width, rank), BF16),
            pltpu.VMEM((LAYERS, 2, members, width, rank), BF16),
            pltpu.VMEM((LAYERS, members, rank // members, 9 * rank), BF16),
            pltpu.VMEM((LAYERS, members, rank // members, 9 * rank), BF16),
            pltpu.VMEM((LAYERS, members, rank // members, 9 * rank), F32),
            dma((5 + 3 * LAYERS, members)),
            dma((5 + 3 * LAYERS, members)),
            dma((2 * LAYERS, 3 * members)),
            dma((2 * LAYERS, 3 * members)),
        ],
        compiler_params=pltpu.CompilerParams(
            collective_id=0, has_side_effects=True, vmem_limit_bytes=48 * 2**20
        ),
    )(
        features, cotangent, down_factor, up_factor, kf, kb, alive, chooser,
        jnp.asarray(border_matrix(), BF16), jnp.asarray(window_matrix(), BF16),
    )
    dgrad, ugrad, cgrad = lax.psum((dgrad, ugrad, cgrad), ("tiles", "sub"))
    cgrad = cgrad.reshape(LAYERS, rank // members, 9, rank).transpose(0, 2, 1, 3)
    return out, dgrad, cgrad, ugrad


def solution(mesh):
    return jax.shard_map(
        functools.partial(local, tuple(mesh.shape[a] for a in ("tiles", "sub", "chan"))),
        mesh=mesh,
        in_specs=(
            P(("groups", "tiles", "sub"), "chan", None),
            P(("groups", "tiles", "sub"), "chan", None),
            P(None, "chan", None),
            P(),
            P(None, "chan", None),
            P(("groups", "tiles", "sub")),
            P(("groups", "tiles", "sub"), None),
            P(("groups", "tiles", "sub"), None),
        ),
        out_specs=(
            P(("groups", "tiles", "sub"), "chan", None),
            P("groups", "chan", None),
            P("groups", None, "chan", None),
            P("groups", "chan", None),
        ),
        check_vma=False,
    )
```

```python
import functools

import jax
import jax.numpy as jnp
import numpy as np
from jax import lax
from jax.experimental import pallas as pl
from jax.experimental.pallas import tpu as pltpu
from jax.sharding import PartitionSpec as P

TILE = 16
PIX = TILE * TILE
LAYERS = 2
HALO = 128
LANE_DIRECTIONS = [(6, 16), (1, 16), (4, 16), (3, 16), (7, 1), (5, 1), (2, 1), (0, 1)]
F32, BF16 = jnp.float32, jnp.bfloat16
MESH = pl.DeviceIdType.MESH


def border_matrix():
    chosen = np.zeros((PIX, HALO), np.float32)
    last = TILE - 1
    for k in range(TILE):
        chosen[k, k] = 1
        chosen[last * TILE + k, TILE + k] = 1
        chosen[k * TILE, 2 * TILE + k] = 1
        chosen[k * TILE + last, 3 * TILE + k] = 1
    for lane, pixel in enumerate((0, last, last * TILE, PIX - 1)):
        chosen[pixel, 4 * TILE + lane] = 1
    return chosen


def window_matrix():
    chosen = np.zeros((PIX + HALO, 9, TILE, TILE), np.float32)
    end = TILE + 1
    for tap in range(9):
        for i in range(TILE):
            for j in range(TILE):
                row, col = i + tap // 3, j + tap % 3
                if 0 < row < end and 0 < col < end:
                    source = (row - 1) * TILE + col - 1
                elif 0 < col < end:
                    source = PIX + (TILE if row == 0 else 0) + col - 1
                elif 0 < row < end:
                    source = PIX + (3 * TILE if col == 0 else 2 * TILE) + row - 1
                else:
                    source = PIX + 4 * TILE + (2 if row == 0 else 0) + (1 if col == 0 else 0)
                chosen[source, tap, i, j] = 1
    return chosen.reshape(PIX + HALO, 9 * PIX)


def nn(a, b):
    return jnp.dot(a, b, preferred_element_type=F32)


def nt(a, b):
    return lax.dot_general(a, b, (((1,), (1,)), ((), ())), preferred_element_type=F32)


def tn(a, b):
    return lax.dot_general(a, b, (((0,), (0,)), ((), ())), preferred_element_type=F32)


def kernel(
    sizes, feat, cot, down, up, kf, kb, alive, chooser, bsel, wsel,
    out, dgrad, ugrad, cgrad,
    inbox, fact, hid, grad_e, zs, bs, wins, mwin, border, ext, stage, outbox, gsend, grecv, csend, crecv, cown,
    dpart, upart, packed, pieces, reduced, whole,
    send_sem, recv_sem, bsend_sem, brecv_sem, rsend_sem, rrecv_sem,
):
    tiles, subs, members, here = sizes
    chan = lax.axis_index("chan")
    owner = lax.axis_index("tiles") * subs + lax.axis_index("sub")
    owners = tiles * subs
    has_prev, has_next = owner > 0, owner < owners - 1
    rank = down.shape[2]
    part = rank // members

    def peer(j):
        return (chan + j) % members

    def at(shift, c):
        o = owner + shift
        return {"tiles": o // subs, "sub": o % subs, "chan": c}

    near = [
        (shift, j, cond)
        for shift, cond in ((0, None), (1, has_next), (-1, has_prev))
        for j in range(members)
        if shift or j
    ]

    def at_owner(o):
        return {"tiles": o // subs, "sub": o % subs}

    def guarded(cond, action):
        if cond is None:
            action()
        else:
            pl.when(cond)(action)

    @pl.when(jnp.logical_not(has_prev))
    def _():
        ext[:, 0] = jnp.zeros_like(ext[:, 0])

    @pl.when(jnp.logical_not(has_next))
    def _():
        ext[:, 2] = jnp.zeros_like(ext[:, 2])

    barrier = pltpu.get_barrier_semaphore()
    for step in range(1, owners):
        pl.semaphore_signal(barrier, inc=1, device_id=at_owner((owner + step) % owners), device_id_type=MESH)
    for shift, j, cond in near:
        if not j:
            continue
        def greet(shift=shift, j=j):
            pl.semaphore_signal(barrier, inc=1, device_id=at(shift, peer(j)), device_id_type=MESH)
        guarded(cond, greet)
    sides = has_prev.astype(jnp.int32) + has_next.astype(jnp.int32)
    pl.semaphore_wait(barrier, owners - 1 + (members - 1) * (1 + sides))

    def to_peer(k, j, src, dst):
        return pltpu.make_async_remote_copy(
            src_ref=src, dst_ref=dst, send_sem=send_sem.at[k, j], recv_sem=recv_sem.at[k, members - j],
            device_id={"chan": peer(j)}, device_id_type=MESH,
        )

    def from_peer(k, j, src, dst):
        return pltpu.make_async_remote_copy(
            src_ref=src, dst_ref=dst, send_sem=send_sem.at[k, j], recv_sem=recv_sem.at[k, j],
            device_id={"chan": peer(j)}, device_id_type=MESH,
        )

    def slots_of(j):
        return pl.ds(peer(j) * here, here)

    peers = range(1, members)
    sent, arrivals = [], {}

    def exchange(k, source, target):
        for j in peers:
            sent.append(to_peer(k, j, source(j), target.at[members - j]))
            sent[-1].start()
        arrivals[k] = [from_peer(k, j, source(j), target.at[j]) for j in peers]

    def arrived(k):
        for copy in arrivals[k]:
            copy.wait_recv()

    exchange(0, lambda j: down, fact.at[0])
    exchange(1, lambda j: feat.at[slots_of(j)], inbox.at[0])
    exchange(2, lambda j: up, fact.at[1])
    exchange(3, lambda j: cot.at[slots_of(j)], inbox.at[1])

    def lanes(x):
        return jnp.concatenate([x[u] for u in range(here)], axis=1)

    def live(x):
        return (lanes(x).astype(F32) * alive[...]).astype(BF16)

    hid[0, 0] = live(feat[slots_of(0)])
    grad_e[0] = live(cot[slots_of(0)])

    def field(factors, blocks):
        total = None
        for factor, block in zip(factors, blocks):
            part = tn(factor, block).astype(BF16).astype(F32)
            total = part if total is None else total + part
        return total.astype(BF16)

    def place(shift, j):
        return shift % 3 * members + j

    def border_copy(r, k):
        shift, j, cond = near[k]
        mirrored = place(-shift, (members - j) % members)
        return cond, pltpu.make_async_remote_copy(
            src_ref=border.at[r], dst_ref=ext.at[r, 1 - shift, chan],
            send_sem=bsend_sem.at[r, place(shift, j)], recv_sem=brecv_sem.at[r, mirrored],
            device_id=at(shift, peer(j)), device_id_type=MESH,
        )

    def border_arrival(r, k):
        shift, j, cond = near[k]
        return cond, pltpu.make_async_remote_copy(
            src_ref=border.at[r], dst_ref=ext.at[r, 1 + shift, peer(j)],
            send_sem=bsend_sem.at[r, place(shift, j)], recv_sem=brecv_sem.at[r, place(shift, j)],
            device_id=at(shift, peer(j)), device_id_type=MESH,
        )

    def send_border(r, rows):
        edge = nn(rows, bsel[...]).astype(BF16).reshape(here, rank, HALO)
        border[r] = edge
        for k in range(len(near)):
            cond, copy = border_copy(r, k)
            guarded(cond, copy.start)
        ext[r, 1, pl.ds(chan, 1)] = edge[None]

    def finish_border(r):
        for k in range(len(near)):
            cond, copy = border_arrival(r, k)
            guarded(cond, copy.wait_recv)

    def drain_border(r):
        for k in range(len(near)):
            cond, copy = border_copy(r, k)
            guarded(cond, copy.wait_send)

    def rows_of(value):
        return jnp.concatenate([value[:, u * PIX:(u + 1) * PIX] for u in range(here)], axis=0)

    def windows(r, rows, target):
        halos = [jnp.zeros((rank, HALO), F32) for _ in range(here)]
        for v in range(3 * members * here):
            piece = ext[r, v // (members * here), v // here % members, v % here].astype(F32)
            for u in range(here):
                w = u * 3 * members * here + v
                halos[u] = halos[u] + piece * chooser[w:w + 1, :]
        halo = jnp.concatenate(halos, axis=0).astype(BF16)
        both = jnp.concatenate([rows, halo], axis=1)
        for tap in range(9):
            moved = nn(both, wsel[:, tap * PIX:(tap + 1) * PIX]).astype(BF16)
            for u in range(here):
                target[tap * rank:(tap + 1) * rank, u * PIX:(u + 1) * PIX] = moved[u * rank:(u + 1) * rank]

    def scatter(layer):
        for k in range(3):
            arrived(5 + 3 * layer + k)
        down_sum, up_sum = dpart[layer], upart[layer]
        core_sum = cown[layer, pl.ds(chan, 1)][0]
        for j in peers:
            down_sum = down_sum + grecv[layer, 0, j].astype(F32)
            up_sum = up_sum + grecv[layer, 1, j].astype(F32)
            core_sum = core_sum + crecv[layer, j].astype(F32)
        spare = whole.shape[1] * whole.shape[2] - down_sum.shape[0] - 5 * part
        core_sum = jnp.concatenate([core_sum, jnp.zeros((part, rank), F32)], axis=1)
        lines = [jnp.concatenate([down_sum, up_sum], axis=1)]
        lines += [core_sum[:, k * 2 * rank:(k + 1) * 2 * rank] for k in range(5)]
        if spare:
            lines.append(jnp.zeros((spare, 2 * rank), F32))
        packed[layer] = jnp.concatenate(lines, axis=0).astype(BF16).reshape(packed.shape[1:])
        for i in range(1, owners):
            owner_copy(0, layer, i, packed.at[layer, (owner + i) % owners], pieces.at[layer, owners - i]).start()

    def owner_copy(stage_at, layer, i, src, dst, arriving=False):
        return pltpu.make_async_remote_copy(
            src_ref=src, dst_ref=dst, send_sem=rsend_sem.at[stage_at, layer, i],
            recv_sem=rrecv_sem.at[stage_at, layer, i if arriving else owners - i],
            device_id=at_owner((owner + i) % owners), device_id_type=MESH,
        )

    def gather(layer):
        total = packed[layer, pl.ds(owner, 1)][0].astype(F32)
        for i in range(1, owners):
            owner_copy(0, layer, i, reduced.at[layer], pieces.at[layer, i], True).wait_recv()
            total = total + pieces[layer, i].astype(F32)
        total = total.astype(BF16)
        reduced[layer] = total
        whole[layer, pl.ds(owner, 1)] = total[None]
        for i in range(1, owners):
            owner_copy(1, layer, i, reduced.at[layer], whole.at[layer, owner]).start()

    def unpack(layer):
        for i in range(1, owners):
            owner_copy(1, layer, i, reduced.at[layer], whole.at[layer, (owner + i) % owners], True).wait_recv()
        lines = whole[layer].reshape(-1, 2 * rank).astype(F32)
        width = dgrad.shape[1]
        dgrad[layer] = lines[:width, :rank]
        ugrad[layer] = lines[:width, rank:]
        for tap in range(9):
            start = width + tap // 2 * part
            cgrad[layer, tap] = lines[start:start + part, tap % 2 * rank:(tap % 2 + 1) * rank]

    def factors(which, layer):
        own = (down, up)[which]
        return [own[layer]] + [fact[which, j, layer] for j in peers]

    arrived(0)
    arrived(1)
    for j in peers:
        hid[0, j] = live(inbox[0, j])
    for layer in range(LAYERS):
        act = field(factors(0, layer), [hid[layer, j] for j in range(members)])
        rows = rows_of(act)
        send_border(layer, rows)
        finish_border(layer)
        windows(layer, rows, wins.at[layer])
        b = nn(kf[layer], wins[layer]).astype(BF16)
        bs[layer] = b
        if layer == 0:
            arrived(2)
            arrived(3)
            for j in peers:
                grad_e[j] = live(inbox[1, j])
        for j, factor in enumerate(factors(1, layer)):
            z = nn(factor, b)
            zs[layer, j] = z
            if layer < LAYERS - 1:
                silu = z * jax.nn.sigmoid(z)
                hid[layer + 1, j] = (hid[layer, j].astype(F32) + silu).astype(BF16)
    for layer in reversed(range(LAYERS)):
        r = LAYERS + layer
        deltas = []
        for j in range(members):
            z = zs[layer, j]
            sig = jax.nn.sigmoid(z)
            e = grad_e[j].astype(F32)
            deltas.append((e * sig * (1.0 + z * (1.0 - sig))).astype(BF16))
        m = field(factors(1, layer), deltas)
        rows = rows_of(m)
        send_border(r, rows)
        core = nt(m, wins[layer])
        for c in range(members):
            piece = core[c * part:(c + 1) * part]
            cown[layer, c] = piece
            csend[layer, c] = piece.astype(BF16)
        exchange(5 + 3 * layer, lambda j: csend.at[layer, peer(j)], crecv.at[layer])
        upart[layer] = nt(deltas[0], bs[layer])
        for j in peers:
            gsend[layer, 1, j] = nt(deltas[j], bs[layer]).astype(BF16)
        exchange(6 + 3 * layer, lambda j: gsend.at[layer, 1, j], grecv.at[layer, 1])
        if layer < LAYERS - 1:
            scatter(layer + 1)
        finish_border(r)
        windows(r, rows, mwin)
        if layer < LAYERS - 1:
            gather(layer + 1)
        n = nn(kb[layer], mwin[...]).astype(BF16)
        through_factors = factors(0, layer)
        for j in (*peers, 0):
            new_e = (grad_e[j].astype(F32) + nn(through_factors[j], n)).astype(BF16)
            if layer > 0:
                grad_e[j] = new_e
                continue
            for u in range(here):
                tile = new_e[:, u * PIX:(u + 1) * PIX]
                if j:
                    stage[j, u] = tile
                else:
                    out[pl.ds(chan * here + u, 1)] = tile[None]
            if j == members - 1:
                exchange(4, lambda i: stage.at[i], outbox)
        for j in peers:
            gsend[layer, 0, j] = nt(hid[layer, j], n).astype(BF16)
        exchange(7 + 3 * layer, lambda j: gsend.at[layer, 0, j], grecv.at[layer, 0])
        dpart[layer] = nt(hid[layer, 0], n)
    scatter(0)
    arrived(4)
    for j in peers:
        for u in range(here):
            out[pl.ds(peer(j) * here + u, 1)] = outbox[j, u][None]
    for layer in reversed(range(1, LAYERS)):
        unpack(layer)
    gather(0)
    unpack(0)
    for layer in range(LAYERS):
        for i in range(1, owners):
            owner_copy(0, layer, i, packed.at[layer, (owner + i) % owners], pieces.at[layer, i]).wait_send()
            owner_copy(1, layer, i, reduced.at[layer], whole.at[layer, owner]).wait_send()
    for copy in sent:
        copy.wait_send()
    for r in range(2 * LAYERS):
        drain_border(r)


def local(sizes, features, cotangent, down_factor, core_kernel, up_factor, tile_count, neighbour_owner, neighbour_slot):
    tiles, subs, members = sizes
    slots, width, _ = features.shape
    here = slots // members
    rank = down_factor.shape[2]
    device = lax.axis_index(("tiles", "sub"))
    first = lax.axis_index("chan") * here
    owner = lax.dynamic_slice_in_dim(neighbour_owner, first, here, 0)
    slot = lax.dynamic_slice_in_dim(neighbour_slot, first, here, 0)
    row = jnp.where(owner >= 0, (owner - device + 1) * slots + slot, -1)
    lane_row = jnp.concatenate(
        [jnp.broadcast_to(row[:, d:d + 1], (here, n)) for d, n in LANE_DIRECTIONS]
        + [jnp.full((here, HALO - 4 * TILE - 4), -1, jnp.int32)],
        axis=1,
    )
    chooser = (lane_row[:, None, :] == jnp.arange(3 * slots)[None, :, None]).astype(F32).reshape(here * 3 * slots, HALO)
    alive = (first + jnp.arange(here * PIX) // PIX < tile_count[0]).astype(F32)[None]
    kf = core_kernel.transpose(0, 2, 1, 3).reshape(LAYERS, rank, 9 * rank)
    kb = core_kernel[:, ::-1].transpose(0, 3, 1, 2).reshape(LAYERS, rank, 9 * rank)
    pixels = here * PIX
    owners = tiles * subs
    chunk = -(-(width + 5 * (rank // members)) // (16 * owners)) * 16
    vmem = pl.BlockSpec(memory_space=pltpu.VMEM)
    dma = pltpu.SemaphoreType.DMA
    out, dgrad, ugrad, cgrad = pl.pallas_call(
        functools.partial(kernel, (tiles, subs, members, here)),
        out_shape=(
            jax.ShapeDtypeStruct(features.shape, BF16),
            jax.ShapeDtypeStruct((LAYERS, width, rank), F32),
            jax.ShapeDtypeStruct((LAYERS, width, rank), F32),
            jax.ShapeDtypeStruct((LAYERS, 9, rank // members, rank), F32),
        ),
        in_specs=[vmem] * 10,
        out_specs=(vmem,) * 4,
        scratch_shapes=[
            pltpu.VMEM((2, members, here, width, PIX), BF16),
            pltpu.VMEM((2, members, LAYERS, width, rank), BF16),
            pltpu.VMEM((LAYERS, members, width, pixels), BF16),
            pltpu.VMEM((members, width, pixels), BF16),
            pltpu.VMEM((LAYERS, members, width, pixels), F32),
            pltpu.VMEM((LAYERS, rank, pixels), BF16),
            pltpu.VMEM((LAYERS, 9 * rank, pixels), BF16),
            pltpu.VMEM((9 * rank, pixels), BF16),
            pltpu.VMEM((2 * LAYERS, here, rank, HALO), BF16),
            pltpu.VMEM((2 * LAYERS, 3, members, here, rank, HALO), BF16),
            pltpu.VMEM((members, here, width, PIX), BF16),
            pltpu.VMEM((members, here, width, PIX), BF16),
            pltpu.VMEM((LAYERS, 2, members, width, rank), BF16),
            pltpu.VMEM((LAYERS, 2, members, width, rank), BF16),
            pltpu.VMEM((LAYERS, members, rank // members, 9 * rank), BF16),
            pltpu.VMEM((LAYERS, members, rank // members, 9 * rank), BF16),
            pltpu.VMEM((LAYERS, members, rank // members, 9 * rank), F32),
            pltpu.VMEM((LAYERS, width, rank), F32),
            pltpu.VMEM((LAYERS, width, rank), F32),
            pltpu.VMEM((LAYERS, owners, chunk, 2 * rank), BF16),
            pltpu.VMEM((LAYERS, owners, chunk, 2 * rank), BF16),
            pltpu.VMEM((LAYERS, chunk, 2 * rank), BF16),
            pltpu.VMEM((LAYERS, owners, chunk, 2 * rank), BF16),
            dma((5 + 3 * LAYERS, members)),
            dma((5 + 3 * LAYERS, members)),
            dma((2 * LAYERS, 3 * members)),
            dma((2 * LAYERS, 3 * members)),
            dma((2, LAYERS, owners)),
            dma((2, LAYERS, owners)),
        ],
        compiler_params=pltpu.CompilerParams(
            collective_id=0, has_side_effects=True, vmem_limit_bytes=48 * 2**20
        ),
    )(
        features, cotangent, down_factor, up_factor, kf, kb, alive, chooser,
        jnp.asarray(border_matrix(), BF16), jnp.asarray(window_matrix(), BF16),
    )
    return out, dgrad, cgrad, ugrad


def solution(mesh):
    return jax.shard_map(
        functools.partial(local, tuple(mesh.shape[a] for a in ("tiles", "sub", "chan"))),
        mesh=mesh,
        in_specs=(
            P(("groups", "tiles", "sub"), "chan", None),
            P(("groups", "tiles", "sub"), "chan", None),
            P(None, "chan", None),
            P(),
            P(None, "chan", None),
            P(("groups", "tiles", "sub")),
            P(("groups", "tiles", "sub"), None),
            P(("groups", "tiles", "sub"), None),
        ),
        out_specs=(
            P(("groups", "tiles", "sub"), "chan", None),
            P("groups", "chan", None),
            P("groups", None, "chan", None),
            P("groups", "chan", None),
        ),
        check_vma=False,
    )
```

```python
import functools

import jax
import jax.numpy as jnp
import numpy as np
from jax import lax
from jax.experimental import pallas as pl
from jax.experimental.pallas import tpu as pltpu
from jax.sharding import PartitionSpec as P

TILE = 16
PIX = TILE * TILE
LAYERS = 2
HALO = 128
LANE_DIRECTIONS = [(6, 16), (1, 16), (4, 16), (3, 16), (7, 1), (5, 1), (2, 1), (0, 1)]
F32, BF16 = jnp.float32, jnp.bfloat16
MESH = pl.DeviceIdType.MESH


def border_matrix():
    chosen = np.zeros((PIX, HALO), np.float32)
    last = TILE - 1
    for k in range(TILE):
        chosen[k, k] = 1
        chosen[last * TILE + k, TILE + k] = 1
        chosen[k * TILE, 2 * TILE + k] = 1
        chosen[k * TILE + last, 3 * TILE + k] = 1
    for lane, pixel in enumerate((0, last, last * TILE, PIX - 1)):
        chosen[pixel, 4 * TILE + lane] = 1
    return chosen


def window_matrix():
    chosen = np.zeros((PIX + HALO, 9, TILE, TILE), np.float32)
    end = TILE + 1
    for tap in range(9):
        for i in range(TILE):
            for j in range(TILE):
                row, col = i + tap // 3, j + tap % 3
                if 0 < row < end and 0 < col < end:
                    source = (row - 1) * TILE + col - 1
                elif 0 < col < end:
                    source = PIX + (TILE if row == 0 else 0) + col - 1
                elif 0 < row < end:
                    source = PIX + (3 * TILE if col == 0 else 2 * TILE) + row - 1
                else:
                    source = PIX + 4 * TILE + (2 if row == 0 else 0) + (1 if col == 0 else 0)
                chosen[source, tap, i, j] = 1
    return chosen.reshape(PIX + HALO, 9 * PIX)


def nn(a, b):
    return jnp.dot(a, b, preferred_element_type=F32)


def nt(a, b):
    return lax.dot_general(a, b, (((1,), (1,)), ((), ())), preferred_element_type=F32)


def tn(a, b):
    return lax.dot_general(a, b, (((0,), (0,)), ((), ())), preferred_element_type=F32)


def kernel(
    sizes, feat, cot, down, up, taps, alive, chooser, bsel, wsel,
    out, dgrad, ugrad, cgrad,
    inbox, fact, hid, grad_e, zs, bs, wins, mwin, border, ext, stage, outbox, gsend, grecv, csend, crecv, cown,
    dpart, upart, packed, pieces, reduced, whole,
    send_sem, recv_sem, bsend_sem, brecv_sem, rsend_sem, rrecv_sem,
):
    tiles, subs, members, here = sizes
    chan = lax.axis_index("chan")
    owner = lax.axis_index("tiles") * subs + lax.axis_index("sub")
    owners = tiles * subs
    has_prev, has_next = owner > 0, owner < owners - 1
    rank = down.shape[1]
    part = rank // members

    def peer(j):
        return (chan + j) % members

    def at(shift, c):
        o = owner + shift
        return {"tiles": o // subs, "sub": o % subs, "chan": c}

    near = [
        (shift, j, cond)
        for shift, cond in ((0, None), (1, has_next), (-1, has_prev))
        for j in range(members)
        if shift or j
    ]

    def at_owner(o):
        return {"tiles": o // subs, "sub": o % subs}

    def guarded(cond, action):
        if cond is None:
            action()
        else:
            pl.when(cond)(action)

    @pl.when(jnp.logical_not(has_prev))
    def _():
        ext[:, 0] = jnp.zeros_like(ext[:, 0])

    @pl.when(jnp.logical_not(has_next))
    def _():
        ext[:, 2] = jnp.zeros_like(ext[:, 2])

    barrier = pltpu.get_barrier_semaphore()
    for step in range(1, owners):
        pl.semaphore_signal(barrier, inc=1, device_id=at_owner((owner + step) % owners), device_id_type=MESH)
    for shift, j, cond in near:
        if not j:
            continue
        def greet(shift=shift, j=j):
            pl.semaphore_signal(barrier, inc=1, device_id=at(shift, peer(j)), device_id_type=MESH)
        guarded(cond, greet)
    sides = has_prev.astype(jnp.int32) + has_next.astype(jnp.int32)
    pl.semaphore_wait(barrier, owners - 1 + (members - 1) * (1 + sides))

    def to_peer(k, j, src, dst):
        return pltpu.make_async_remote_copy(
            src_ref=src, dst_ref=dst, send_sem=send_sem.at[k, j], recv_sem=recv_sem.at[k, members - j],
            device_id={"chan": peer(j)}, device_id_type=MESH,
        )

    def from_peer(k, j, src, dst):
        return pltpu.make_async_remote_copy(
            src_ref=src, dst_ref=dst, send_sem=send_sem.at[k, j], recv_sem=recv_sem.at[k, j],
            device_id={"chan": peer(j)}, device_id_type=MESH,
        )

    def slots_of(j):
        return pl.ds(peer(j) * here, here)

    peers = range(1, members)
    sent, arrivals = [], {}

    def exchange(k, source, target):
        for j in peers:
            sent.append(to_peer(k, j, source(j), target.at[members - j]))
            sent[-1].start()
        arrivals[k] = [from_peer(k, j, source(j), target.at[j]) for j in peers]

    def arrived(k):
        for copy in arrivals[k]:
            copy.wait_recv()

    exchange(0, lambda j: down, fact.at[0])
    exchange(1, lambda j: feat.at[slots_of(j)], inbox.at[0])
    exchange(2, lambda j: up, fact.at[1])
    exchange(3, lambda j: cot.at[slots_of(j)], inbox.at[1])

    def lanes(x):
        return jnp.concatenate([x[u] for u in range(here)], axis=1)

    def live(x):
        return (lanes(x).astype(F32) * alive[...]).astype(BF16)

    hid[0, 0] = live(feat[slots_of(0)])
    grad_e[0] = live(cot[slots_of(0)])

    def field(factors, blocks):
        total = None
        for factor, block in zip(factors, blocks):
            part = nn(factor, block).astype(BF16).astype(F32)
            total = part if total is None else total + part
        return total.astype(BF16)

    def place(shift, j):
        return shift % 3 * members + j

    def border_copy(r, k):
        shift, j, cond = near[k]
        mirrored = place(-shift, (members - j) % members)
        return cond, pltpu.make_async_remote_copy(
            src_ref=border.at[r], dst_ref=ext.at[r, 1 - shift, chan],
            send_sem=bsend_sem.at[r, place(shift, j)], recv_sem=brecv_sem.at[r, mirrored],
            device_id=at(shift, peer(j)), device_id_type=MESH,
        )

    def border_arrival(r, k):
        shift, j, cond = near[k]
        return cond, pltpu.make_async_remote_copy(
            src_ref=border.at[r], dst_ref=ext.at[r, 1 + shift, peer(j)],
            send_sem=bsend_sem.at[r, place(shift, j)], recv_sem=brecv_sem.at[r, place(shift, j)],
            device_id=at(shift, peer(j)), device_id_type=MESH,
        )

    def send_border(r, rows):
        edge = nn(rows, bsel[...]).astype(BF16).reshape(here, rank, HALO)
        border[r] = edge
        for k in range(len(near)):
            cond, copy = border_copy(r, k)
            guarded(cond, copy.start)
        ext[r, 1, pl.ds(chan, 1)] = edge[None]

    def finish_border(r):
        for k in range(len(near)):
            cond, copy = border_arrival(r, k)
            guarded(cond, copy.wait_recv)

    def drain_border(r):
        for k in range(len(near)):
            cond, copy = border_copy(r, k)
            guarded(cond, copy.wait_send)

    def rows_of(value):
        return jnp.concatenate([value[:, u * PIX:(u + 1) * PIX] for u in range(here)], axis=0)

    def windows(r, rows, target, flipped=False):
        halos = [jnp.zeros((rank, HALO), F32) for _ in range(here)]
        for v in range(3 * members * here):
            piece = ext[r, v // (members * here), v // here % members, v % here].astype(F32)
            for u in range(here):
                w = u * 3 * members * here + v
                halos[u] = halos[u] + piece * chooser[w:w + 1, :]
        halo = jnp.concatenate(halos, axis=0).astype(BF16)
        both = jnp.concatenate([rows, halo], axis=1)
        for tap in range(9):
            moved = nn(both, wsel[:, tap * PIX:(tap + 1) * PIX]).astype(BF16)
            for u in range(here):
                to = 8 - tap if flipped else tap
                target[to * rank:(to + 1) * rank, u * PIX:(u + 1) * PIX] = moved[u * rank:(u + 1) * rank]

    def scatter(layer):
        for k in range(3):
            arrived(5 + 3 * layer + k)
        down_sum, up_sum = dpart[layer], upart[layer]
        core_sum = cown[layer, pl.ds(chan, 1)][0]
        for j in peers:
            down_sum = down_sum + grecv[layer, 0, j].astype(F32)
            up_sum = up_sum + grecv[layer, 1, j].astype(F32)
            core_sum = core_sum + crecv[layer, j].astype(F32)
        width = down_sum.shape[1]
        spare = whole.shape[1] * whole.shape[2] - width - 5 * part
        core_sum = jnp.concatenate([core_sum, jnp.zeros((part, rank), F32)], axis=1)
        factor_sums = jnp.concatenate([down_sum, up_sum], axis=1)
        lines = [factor_sums[:, k * 2 * rank:(k + 1) * 2 * rank] for k in range(width // rank)]
        lines += [core_sum[:, k * 2 * rank:(k + 1) * 2 * rank] for k in range(5)]
        if spare:
            lines.append(jnp.zeros((spare, 2 * rank), F32))
        packed[layer] = jnp.concatenate(lines, axis=0).astype(BF16).reshape(packed.shape[1:])
        for i in range(1, owners):
            owner_copy(0, layer, i, packed.at[layer, (owner + i) % owners], pieces.at[layer, owners - i]).start()

    def owner_copy(stage_at, layer, i, src, dst, arriving=False):
        return pltpu.make_async_remote_copy(
            src_ref=src, dst_ref=dst, send_sem=rsend_sem.at[stage_at, layer, i],
            recv_sem=rrecv_sem.at[stage_at, layer, i if arriving else owners - i],
            device_id=at_owner((owner + i) % owners), device_id_type=MESH,
        )

    def gather(layer):
        total = packed[layer, pl.ds(owner, 1)][0].astype(F32)
        for i in range(1, owners):
            owner_copy(0, layer, i, reduced.at[layer], pieces.at[layer, i], True).wait_recv()
            total = total + pieces[layer, i].astype(F32)
        total = total.astype(BF16)
        reduced[layer] = total
        whole[layer, pl.ds(owner, 1)] = total[None]
        for i in range(1, owners):
            owner_copy(1, layer, i, reduced.at[layer], whole.at[layer, owner]).start()

    def unpack(layer):
        for i in range(1, owners):
            owner_copy(1, layer, i, reduced.at[layer], whole.at[layer, (owner + i) % owners], True).wait_recv()
        lines = whole[layer].reshape(-1, 2 * rank).astype(F32)
        width = dgrad.shape[2]
        both = jnp.concatenate([lines[k * rank:(k + 1) * rank] for k in range(width // rank)], axis=1)
        dgrad[layer] = both[:, :width]
        ugrad[layer] = both[:, width:]
        for tap in range(9):
            start = width + tap // 2 * part
            cgrad[layer, tap] = lines[start:start + part, tap % 2 * rank:(tap % 2 + 1) * rank]

    def factors(which, layer):
        own = (down, up)[which]
        return [own[layer]] + [fact[which, j, layer] for j in peers]

    arrived(0)
    arrived(1)
    for j in peers:
        hid[0, j] = live(inbox[0, j])
    for layer in range(LAYERS):
        act = field(factors(0, layer), [hid[layer, j] for j in range(members)])
        rows = rows_of(act)
        send_border(layer, rows)
        finish_border(layer)
        windows(layer, rows, wins.at[layer])
        mixer = jnp.concatenate([taps[layer, tap] for tap in range(9)], axis=1)
        b = nn(mixer, wins[layer]).astype(BF16)
        bs[layer] = b
        if layer == 0:
            arrived(2)
            arrived(3)
            for j in peers:
                grad_e[j] = live(inbox[1, j])
        for j, factor in enumerate(factors(1, layer)):
            z = tn(factor, b)
            zs[layer, j] = z
            if layer < LAYERS - 1:
                silu = z * jax.nn.sigmoid(z)
                hid[layer + 1, j] = (hid[layer, j].astype(F32) + silu).astype(BF16)
    for layer in reversed(range(LAYERS)):
        r = LAYERS + layer
        deltas = []
        for j in range(members):
            z = zs[layer, j]
            sig = jax.nn.sigmoid(z)
            e = grad_e[j].astype(F32)
            deltas.append((e * sig * (1.0 + z * (1.0 - sig))).astype(BF16))
        m = field(factors(1, layer), deltas)
        rows = rows_of(m)
        send_border(r, rows)
        core = nt(m, wins[layer])
        for c in range(members):
            piece = core[c * part:(c + 1) * part]
            cown[layer, c] = piece
            csend[layer, c] = piece.astype(BF16)
        exchange(5 + 3 * layer, lambda j: csend.at[layer, peer(j)], crecv.at[layer])
        upart[layer] = nt(bs[layer], deltas[0])
        for j in peers:
            gsend[layer, 1, j] = nt(bs[layer], deltas[j]).astype(BF16)
        exchange(6 + 3 * layer, lambda j: gsend.at[layer, 1, j], grecv.at[layer, 1])
        if layer < LAYERS - 1:
            scatter(layer + 1)
        finish_border(r)
        windows(r, rows, mwin, True)
        if layer < LAYERS - 1:
            gather(layer + 1)
        n = tn(taps[layer].reshape(9 * rank, rank), mwin[...]).astype(BF16)
        through_factors = factors(0, layer)
        for j in (*peers, 0):
            new_e = (grad_e[j].astype(F32) + tn(through_factors[j], n)).astype(BF16)
            if layer > 0:
                grad_e[j] = new_e
                continue
            for u in range(here):
                tile = new_e[:, u * PIX:(u + 1) * PIX]
                if j:
                    stage[j, u] = tile
                else:
                    out[pl.ds(chan * here + u, 1)] = tile[None]
            if j == members - 1:
                exchange(4, lambda i: stage.at[i], outbox)
        for j in peers:
            gsend[layer, 0, j] = nt(n, hid[layer, j]).astype(BF16)
        exchange(7 + 3 * layer, lambda j: gsend.at[layer, 0, j], grecv.at[layer, 0])
        dpart[layer] = nt(n, hid[layer, 0])
    scatter(0)
    arrived(4)
    for j in peers:
        for u in range(here):
            out[pl.ds(peer(j) * here + u, 1)] = outbox[j, u][None]
    for layer in reversed(range(1, LAYERS)):
        unpack(layer)
    gather(0)
    unpack(0)
    for layer in range(LAYERS):
        for i in range(1, owners):
            owner_copy(0, layer, i, packed.at[layer, (owner + i) % owners], pieces.at[layer, i]).wait_send()
            owner_copy(1, layer, i, reduced.at[layer], whole.at[layer, owner]).wait_send()
    for copy in sent:
        copy.wait_send()
    for r in range(2 * LAYERS):
        drain_border(r)


def local(sizes, features, cotangent, down_factor, core_kernel, up_factor, tile_count, neighbour_owner, neighbour_slot):
    tiles, subs, members = sizes
    slots, width, _ = features.shape
    here = slots // members
    rank = down_factor.shape[2]
    device = lax.axis_index(("tiles", "sub"))
    first = lax.axis_index("chan") * here
    owner = lax.dynamic_slice_in_dim(neighbour_owner, first, here, 0)
    slot = lax.dynamic_slice_in_dim(neighbour_slot, first, here, 0)
    row = jnp.where(owner >= 0, (owner - device + 1) * slots + slot, -1)
    lane_row = jnp.concatenate(
        [jnp.broadcast_to(row[:, d:d + 1], (here, n)) for d, n in LANE_DIRECTIONS]
        + [jnp.full((here, HALO - 4 * TILE - 4), -1, jnp.int32)],
        axis=1,
    )
    chooser = (lane_row[:, None, :] == jnp.arange(3 * slots)[None, :, None]).astype(F32).reshape(here * 3 * slots, HALO)
    alive = (first + jnp.arange(here * PIX) // PIX < tile_count[0]).astype(F32)[None]
    pixels = here * PIX
    owners = tiles * subs
    chunk = -(-(width + 5 * (rank // members)) // (16 * owners)) * 16
    vmem = pl.BlockSpec(memory_space=pltpu.VMEM)
    dma = pltpu.SemaphoreType.DMA
    out, dgrad, ugrad, cgrad = pl.pallas_call(
        functools.partial(kernel, (tiles, subs, members, here)),
        out_shape=(
            jax.ShapeDtypeStruct(features.shape, BF16),
            jax.ShapeDtypeStruct((LAYERS, rank, width), F32),
            jax.ShapeDtypeStruct((LAYERS, rank, width), F32),
            jax.ShapeDtypeStruct((LAYERS, 9, rank // members, rank), F32),
        ),
        in_specs=[vmem] * 9,
        out_specs=(vmem,) * 4,
        scratch_shapes=[
            pltpu.VMEM((2, members, here, width, PIX), BF16),
            pltpu.VMEM((2, members, LAYERS, rank, width), BF16),
            pltpu.VMEM((LAYERS, members, width, pixels), BF16),
            pltpu.VMEM((members, width, pixels), BF16),
            pltpu.VMEM((LAYERS, members, width, pixels), F32),
            pltpu.VMEM((LAYERS, rank, pixels), BF16),
            pltpu.VMEM((LAYERS, 9 * rank, pixels), BF16),
            pltpu.VMEM((9 * rank, pixels), BF16),
            pltpu.VMEM((2 * LAYERS, here, rank, HALO), BF16),
            pltpu.VMEM((2 * LAYERS, 3, members, here, rank, HALO), BF16),
            pltpu.VMEM((members, here, width, PIX), BF16),
            pltpu.VMEM((members, here, width, PIX), BF16),
            pltpu.VMEM((LAYERS, 2, members, rank, width), BF16),
            pltpu.VMEM((LAYERS, 2, members, rank, width), BF16),
            pltpu.VMEM((LAYERS, members, rank // members, 9 * rank), BF16),
            pltpu.VMEM((LAYERS, members, rank // members, 9 * rank), BF16),
            pltpu.VMEM((LAYERS, members, rank // members, 9 * rank), F32),
            pltpu.VMEM((LAYERS, rank, width), F32),
            pltpu.VMEM((LAYERS, rank, width), F32),
            pltpu.VMEM((LAYERS, owners, chunk, 2 * rank), BF16),
            pltpu.VMEM((LAYERS, owners, chunk, 2 * rank), BF16),
            pltpu.VMEM((LAYERS, chunk, 2 * rank), BF16),
            pltpu.VMEM((LAYERS, owners, chunk, 2 * rank), BF16),
            dma((5 + 3 * LAYERS, members)),
            dma((5 + 3 * LAYERS, members)),
            dma((2 * LAYERS, 3 * members)),
            dma((2 * LAYERS, 3 * members)),
            dma((2, LAYERS, owners)),
            dma((2, LAYERS, owners)),
        ],
        compiler_params=pltpu.CompilerParams(
            collective_id=0, has_side_effects=True, vmem_limit_bytes=48 * 2**20
        ),
    )(
        features, cotangent, down_factor.transpose(0, 2, 1), up_factor.transpose(0, 2, 1), core_kernel, alive, chooser,
        jnp.asarray(border_matrix(), BF16), jnp.asarray(window_matrix(), BF16),
    )
    return out, dgrad.transpose(0, 2, 1), cgrad, ugrad.transpose(0, 2, 1)


def solution(mesh):
    return jax.shard_map(
        functools.partial(local, tuple(mesh.shape[a] for a in ("tiles", "sub", "chan"))),
        mesh=mesh,
        in_specs=(
            P(("groups", "tiles", "sub"), "chan", None),
            P(("groups", "tiles", "sub"), "chan", None),
            P(None, "chan", None),
            P(),
            P(None, "chan", None),
            P(("groups", "tiles", "sub")),
            P(("groups", "tiles", "sub"), None),
            P(("groups", "tiles", "sub"), None),
        ),
        out_specs=(
            P(("groups", "tiles", "sub"), "chan", None),
            P("groups", "chan", None),
            P("groups", None, "chan", None),
            P("groups", "chan", None),
        ),
        check_vma=False,
    )
```

```python
import functools

import jax
import jax.numpy as jnp
import numpy as np
from jax import lax
from jax.experimental import pallas as pl
from jax.experimental.pallas import tpu as pltpu
from jax.sharding import PartitionSpec as P

TILE = 16
PIX = TILE * TILE
LAYERS = 2
HALO = 128
LANE_DIRECTIONS = [(6, 16), (1, 16), (4, 16), (3, 16), (7, 1), (5, 1), (2, 1), (0, 1)]
F32, BF16 = jnp.float32, jnp.bfloat16
MESH = pl.DeviceIdType.MESH


def border_matrix():
    chosen = np.zeros((PIX, HALO), np.float32)
    last = TILE - 1
    for k in range(TILE):
        chosen[k, k] = 1
        chosen[last * TILE + k, TILE + k] = 1
        chosen[k * TILE, 2 * TILE + k] = 1
        chosen[k * TILE + last, 3 * TILE + k] = 1
    for lane, pixel in enumerate((0, last, last * TILE, PIX - 1)):
        chosen[pixel, 4 * TILE + lane] = 1
    return chosen


def window_matrix():
    chosen = np.zeros((PIX + HALO, 9, TILE, TILE), np.float32)
    end = TILE + 1
    for tap in range(9):
        for i in range(TILE):
            for j in range(TILE):
                row, col = i + tap // 3, j + tap % 3
                if 0 < row < end and 0 < col < end:
                    source = (row - 1) * TILE + col - 1
                elif 0 < col < end:
                    source = PIX + (TILE if row == 0 else 0) + col - 1
                elif 0 < row < end:
                    source = PIX + (3 * TILE if col == 0 else 2 * TILE) + row - 1
                else:
                    source = PIX + 4 * TILE + (2 if row == 0 else 0) + (1 if col == 0 else 0)
                chosen[source, tap, i, j] = 1
    return chosen.reshape(PIX + HALO, 9 * PIX)


def nn(a, b):
    return jnp.dot(a, b, preferred_element_type=F32)


def nt(a, b):
    return lax.dot_general(a, b, (((1,), (1,)), ((), ())), preferred_element_type=F32)


def tn(a, b):
    return lax.dot_general(a, b, (((0,), (0,)), ((), ())), preferred_element_type=F32)


def kernel(
    sizes, feat, cot, down, up, taps, alive, chooser, bsel, wsel_far,
    out, dgrad, ugrad, cgrad,
    inbox, fact, hid, grad_e, zs, bs, wins, mwin, border, ext, stage, outbox, gsend, grecv, csend, crecv, cown,
    dpart, upart, packed, pieces, reduced, whole,
    send_sem, recv_sem, bsend_sem, brecv_sem, rsend_sem, rrecv_sem, wsel, local_sem,
):
    tiles, subs, members, here = sizes
    chan = lax.axis_index("chan")
    owner = lax.axis_index("tiles") * subs + lax.axis_index("sub")
    owners = tiles * subs
    has_prev, has_next = owner > 0, owner < owners - 1
    rank = down.shape[1]
    part = rank // members

    def peer(j):
        return (chan + j) % members

    def at(shift, c):
        o = owner + shift
        return {"tiles": o // subs, "sub": o % subs, "chan": c}

    near = [
        (shift, j, cond)
        for shift, cond in ((0, None), (1, has_next), (-1, has_prev))
        for j in range(members)
        if shift or j
    ]

    def at_owner(o):
        return {"tiles": o // subs, "sub": o % subs}

    def guarded(cond, action):
        if cond is None:
            action()
        else:
            pl.when(cond)(action)

    def slots_of(j):
        return pl.ds(peer(j) * here, here)

    own_copies = [
        pltpu.make_async_copy(feat.at[slots_of(0)], inbox.at[0, 0], local_sem.at[0]),
        pltpu.make_async_copy(cot.at[slots_of(0)], inbox.at[1, 0], local_sem.at[1]),
        pltpu.make_async_copy(wsel_far, wsel, local_sem.at[2]),
    ]
    for copy in own_copies:
        copy.start()

    @pl.when(jnp.logical_not(has_prev))
    def _():
        ext[:, 0] = jnp.zeros_like(ext[:, 0])

    @pl.when(jnp.logical_not(has_next))
    def _():
        ext[:, 2] = jnp.zeros_like(ext[:, 2])

    barrier = pltpu.get_barrier_semaphore()
    for step in range(1, owners):
        pl.semaphore_signal(barrier, inc=1, device_id=at_owner((owner + step) % owners), device_id_type=MESH)
    for shift, j, cond in near:
        if not j:
            continue
        def greet(shift=shift, j=j):
            pl.semaphore_signal(barrier, inc=1, device_id=at(shift, peer(j)), device_id_type=MESH)
        guarded(cond, greet)
    sides = has_prev.astype(jnp.int32) + has_next.astype(jnp.int32)
    pl.semaphore_wait(barrier, owners - 1 + (members - 1) * (1 + sides))

    def to_peer(k, j, src, dst):
        return pltpu.make_async_remote_copy(
            src_ref=src, dst_ref=dst, send_sem=send_sem.at[k, j], recv_sem=recv_sem.at[k, members - j],
            device_id={"chan": peer(j)}, device_id_type=MESH,
        )

    def from_peer(k, j, src, dst):
        return pltpu.make_async_remote_copy(
            src_ref=src, dst_ref=dst, send_sem=send_sem.at[k, j], recv_sem=recv_sem.at[k, j],
            device_id={"chan": peer(j)}, device_id_type=MESH,
        )

    peers = range(1, members)
    sent, arrivals = [], {}

    def exchange(k, source, target):
        for j in peers:
            sent.append(to_peer(k, j, source(j), target.at[members - j]))
            sent[-1].start()
        arrivals[k] = [from_peer(k, j, source(j), target.at[j]) for j in peers]

    def arrived(k):
        for copy in arrivals[k]:
            copy.wait_recv()

    exchange(0, lambda j: down, fact.at[0])
    exchange(1, lambda j: feat.at[slots_of(j)], inbox.at[0])
    exchange(2, lambda j: up, fact.at[1])
    exchange(3, lambda j: cot.at[slots_of(j)], inbox.at[1])

    def lanes(x):
        return jnp.concatenate([x[u] for u in range(here)], axis=1)

    def live(x):
        return (lanes(x).astype(F32) * alive[...]).astype(BF16)

    for copy in own_copies:
        copy.wait()
    hid[0, 0] = live(inbox[0, 0])
    grad_e[0] = live(inbox[1, 0])

    def field(factors, blocks):
        total = None
        for factor, block in zip(factors, blocks):
            part = nn(factor, block).astype(BF16).astype(F32)
            total = part if total is None else total + part
        return total.astype(BF16)

    def place(shift, j):
        return shift % 3 * members + j

    def border_copy(r, k):
        shift, j, cond = near[k]
        mirrored = place(-shift, (members - j) % members)
        return cond, pltpu.make_async_remote_copy(
            src_ref=border.at[r], dst_ref=ext.at[r, 1 - shift, chan],
            send_sem=bsend_sem.at[r, place(shift, j)], recv_sem=brecv_sem.at[r, mirrored],
            device_id=at(shift, peer(j)), device_id_type=MESH,
        )

    def border_arrival(r, k):
        shift, j, cond = near[k]
        return cond, pltpu.make_async_remote_copy(
            src_ref=border.at[r], dst_ref=ext.at[r, 1 + shift, peer(j)],
            send_sem=bsend_sem.at[r, place(shift, j)], recv_sem=brecv_sem.at[r, place(shift, j)],
            device_id=at(shift, peer(j)), device_id_type=MESH,
        )

    def send_border(r, rows):
        edge = nn(rows, bsel[...]).astype(BF16).reshape(here, rank, HALO)
        border[r] = edge
        for k in range(len(near)):
            cond, copy = border_copy(r, k)
            guarded(cond, copy.start)
        ext[r, 1, pl.ds(chan, 1)] = edge[None]

    def finish_border(r):
        for k in range(len(near)):
            cond, copy = border_arrival(r, k)
            guarded(cond, copy.wait_recv)

    def drain_border(r):
        for k in range(len(near)):
            cond, copy = border_copy(r, k)
            guarded(cond, copy.wait_send)

    def rows_of(value):
        return jnp.concatenate([value[:, u * PIX:(u + 1) * PIX] for u in range(here)], axis=0)

    def windows(r, rows, target, flipped=False):
        halos = [jnp.zeros((rank, HALO), F32) for _ in range(here)]
        for v in range(3 * members * here):
            piece = ext[r, v // (members * here), v // here % members, v % here].astype(F32)
            for u in range(here):
                w = u * 3 * members * here + v
                halos[u] = halos[u] + piece * chooser[w:w + 1, :]
        halo = jnp.concatenate(halos, axis=0).astype(BF16)
        both = jnp.concatenate([rows, halo], axis=1)
        for tap in range(9):
            moved = nn(both, wsel[:, tap * PIX:(tap + 1) * PIX]).astype(BF16)
            for u in range(here):
                to = 8 - tap if flipped else tap
                target[to * rank:(to + 1) * rank, u * PIX:(u + 1) * PIX] = moved[u * rank:(u + 1) * rank]

    def scatter(layer):
        for k in range(3):
            arrived(5 + 3 * layer + k)
        down_sum, up_sum = dpart[layer], upart[layer]
        core_sum = cown[layer, pl.ds(chan, 1)][0]
        for j in peers:
            down_sum = down_sum + grecv[layer, 0, j].astype(F32)
            up_sum = up_sum + grecv[layer, 1, j].astype(F32)
            core_sum = core_sum + crecv[layer, j].astype(F32)
        width = down_sum.shape[1]
        spare = whole.shape[1] * whole.shape[2] - width - 5 * part
        core_sum = jnp.concatenate([core_sum, jnp.zeros((part, rank), F32)], axis=1)
        factor_sums = jnp.concatenate([down_sum, up_sum], axis=1)
        lines = [factor_sums[:, k * 2 * rank:(k + 1) * 2 * rank] for k in range(width // rank)]
        lines += [core_sum[:, k * 2 * rank:(k + 1) * 2 * rank] for k in range(5)]
        if spare:
            lines.append(jnp.zeros((spare, 2 * rank), F32))
        packed[layer] = jnp.concatenate(lines, axis=0).astype(BF16).reshape(packed.shape[1:])
        for i in range(1, owners):
            owner_copy(0, layer, i, packed.at[layer, (owner + i) % owners], pieces.at[layer, owners - i]).start()

    def owner_copy(stage_at, layer, i, src, dst, arriving=False):
        return pltpu.make_async_remote_copy(
            src_ref=src, dst_ref=dst, send_sem=rsend_sem.at[stage_at, layer, i],
            recv_sem=rrecv_sem.at[stage_at, layer, i if arriving else owners - i],
            device_id=at_owner((owner + i) % owners), device_id_type=MESH,
        )

    def gather(layer):
        total = packed[layer, pl.ds(owner, 1)][0].astype(F32)
        for i in range(1, owners):
            owner_copy(0, layer, i, reduced.at[layer], pieces.at[layer, i], True).wait_recv()
            total = total + pieces[layer, i].astype(F32)
        total = total.astype(BF16)
        reduced[layer] = total
        whole[layer, pl.ds(owner, 1)] = total[None]
        for i in range(1, owners):
            owner_copy(1, layer, i, reduced.at[layer], whole.at[layer, owner]).start()

    def unpack(layer):
        for i in range(1, owners):
            owner_copy(1, layer, i, reduced.at[layer], whole.at[layer, (owner + i) % owners], True).wait_recv()
        lines = whole[layer].reshape(-1, 2 * rank).astype(F32)
        width = dgrad.shape[2]
        both = jnp.concatenate([lines[k * rank:(k + 1) * rank] for k in range(width // rank)], axis=1)
        dgrad[layer] = both[:, :width]
        ugrad[layer] = both[:, width:]
        for tap in range(9):
            start = width + tap // 2 * part
            cgrad[layer, tap] = lines[start:start + part, tap % 2 * rank:(tap % 2 + 1) * rank]

    def factors(which, layer):
        own = (down, up)[which]
        return [own[layer]] + [fact[which, j, layer] for j in peers]

    arrived(0)
    arrived(1)
    for j in peers:
        hid[0, j] = live(inbox[0, j])
    for layer in range(LAYERS):
        act = field(factors(0, layer), [hid[layer, j] for j in range(members)])
        rows = rows_of(act)
        send_border(layer, rows)
        finish_border(layer)
        windows(layer, rows, wins.at[layer])
        mixer = jnp.concatenate([taps[layer, tap] for tap in range(9)], axis=1)
        b = nn(mixer, wins[layer]).astype(BF16)
        bs[layer] = b
        if layer == 0:
            arrived(2)
            arrived(3)
            for j in peers:
                grad_e[j] = live(inbox[1, j])
        for j, factor in enumerate(factors(1, layer)):
            z = tn(factor, b)
            zs[layer, j] = z
            if layer < LAYERS - 1:
                silu = z * jax.nn.sigmoid(z)
                hid[layer + 1, j] = (hid[layer, j].astype(F32) + silu).astype(BF16)
    for layer in reversed(range(LAYERS)):
        r = LAYERS + layer
        deltas = []
        for j in range(members):
            z = zs[layer, j]
            sig = jax.nn.sigmoid(z)
            e = grad_e[j].astype(F32)
            deltas.append((e * sig * (1.0 + z * (1.0 - sig))).astype(BF16))
        m = field(factors(1, layer), deltas)
        rows = rows_of(m)
        send_border(r, rows)
        core = nt(m, wins[layer])
        for c in range(members):
            piece = core[c * part:(c + 1) * part]
            cown[layer, c] = piece
            csend[layer, c] = piece.astype(BF16)
        exchange(5 + 3 * layer, lambda j: csend.at[layer, peer(j)], crecv.at[layer])
        upart[layer] = nt(bs[layer], deltas[0])
        for j in peers:
            gsend[layer, 1, j] = nt(bs[layer], deltas[j]).astype(BF16)
        exchange(6 + 3 * layer, lambda j: gsend.at[layer, 1, j], grecv.at[layer, 1])
        if layer < LAYERS - 1:
            scatter(layer + 1)
        finish_border(r)
        windows(r, rows, mwin, True)
        if layer < LAYERS - 1:
            gather(layer + 1)
        n = tn(taps[layer].reshape(9 * rank, rank), mwin[...]).astype(BF16)
        through_factors = factors(0, layer)
        for j in (*peers, 0):
            new_e = (grad_e[j].astype(F32) + tn(through_factors[j], n)).astype(BF16)
            if layer > 0:
                grad_e[j] = new_e
                continue
            for u in range(here):
                tile = new_e[:, u * PIX:(u + 1) * PIX]
                if j:
                    stage[j, u] = tile
                else:
                    out[pl.ds(chan * here + u, 1)] = tile[None]
            if j == members - 1:
                exchange(4, lambda i: stage.at[i], outbox)
        for j in peers:
            gsend[layer, 0, j] = nt(n, hid[layer, j]).astype(BF16)
        exchange(7 + 3 * layer, lambda j: gsend.at[layer, 0, j], grecv.at[layer, 0])
        dpart[layer] = nt(n, hid[layer, 0])
    scatter(0)
    arrived(4)
    for j in peers:
        for u in range(here):
            out[pl.ds(peer(j) * here + u, 1)] = outbox[j, u][None]
    for layer in reversed(range(1, LAYERS)):
        unpack(layer)
    gather(0)
    unpack(0)
    for layer in range(LAYERS):
        for i in range(1, owners):
            owner_copy(0, layer, i, packed.at[layer, (owner + i) % owners], pieces.at[layer, i]).wait_send()
            owner_copy(1, layer, i, reduced.at[layer], whole.at[layer, owner]).wait_send()
    for copy in sent:
        copy.wait_send()
    for r in range(2 * LAYERS):
        drain_border(r)


def local(sizes, features, cotangent, down_factor, core_kernel, up_factor, tile_count, neighbour_owner, neighbour_slot):
    tiles, subs, members = sizes
    slots, width, _ = features.shape
    here = slots // members
    rank = down_factor.shape[2]
    device = lax.axis_index(("tiles", "sub"))
    first = lax.axis_index("chan") * here
    owner = lax.dynamic_slice_in_dim(neighbour_owner, first, here, 0)
    slot = lax.dynamic_slice_in_dim(neighbour_slot, first, here, 0)
    row = jnp.where(owner >= 0, (owner - device + 1) * slots + slot, -1)
    lane_row = jnp.concatenate(
        [jnp.broadcast_to(row[:, d:d + 1], (here, n)) for d, n in LANE_DIRECTIONS]
        + [jnp.full((here, HALO - 4 * TILE - 4), -1, jnp.int32)],
        axis=1,
    )
    chooser = (lane_row[:, None, :] == jnp.arange(3 * slots)[None, :, None]).astype(F32).reshape(here * 3 * slots, HALO)
    alive = (first + jnp.arange(here * PIX) // PIX < tile_count[0]).astype(F32)[None]
    pixels = here * PIX
    owners = tiles * subs
    chunk = -(-(width + 5 * (rank // members)) // (16 * owners)) * 16
    vmem = pl.BlockSpec(memory_space=pltpu.VMEM)
    far = pl.BlockSpec(memory_space=pltpu.HBM)
    dma = pltpu.SemaphoreType.DMA
    out, dgrad, ugrad, cgrad = pl.pallas_call(
        functools.partial(kernel, (tiles, subs, members, here)),
        out_shape=(
            jax.ShapeDtypeStruct(features.shape, BF16),
            jax.ShapeDtypeStruct((LAYERS, rank, width), F32),
            jax.ShapeDtypeStruct((LAYERS, rank, width), F32),
            jax.ShapeDtypeStruct((LAYERS, 9, rank // members, rank), F32),
        ),
        in_specs=[far, far] + [vmem] * 6 + [far],
        out_specs=(vmem,) * 4,
        scratch_shapes=[
            pltpu.VMEM((2, members, here, width, PIX), BF16),
            pltpu.VMEM((2, members, LAYERS, rank, width), BF16),
            pltpu.VMEM((LAYERS, members, width, pixels), BF16),
            pltpu.VMEM((members, width, pixels), BF16),
            pltpu.VMEM((LAYERS, members, width, pixels), F32),
            pltpu.VMEM((LAYERS, rank, pixels), BF16),
            pltpu.VMEM((LAYERS, 9 * rank, pixels), BF16),
            pltpu.VMEM((9 * rank, pixels), BF16),
            pltpu.VMEM((2 * LAYERS, here, rank, HALO), BF16),
            pltpu.VMEM((2 * LAYERS, 3, members, here, rank, HALO), BF16),
            pltpu.VMEM((members, here, width, PIX), BF16),
            pltpu.VMEM((members, here, width, PIX), BF16),
            pltpu.VMEM((LAYERS, 2, members, rank, width), BF16),
            pltpu.VMEM((LAYERS, 2, members, rank, width), BF16),
            pltpu.VMEM((LAYERS, members, rank // members, 9 * rank), BF16),
            pltpu.VMEM((LAYERS, members, rank // members, 9 * rank), BF16),
            pltpu.VMEM((LAYERS, members, rank // members, 9 * rank), F32),
            pltpu.VMEM((LAYERS, rank, width), F32),
            pltpu.VMEM((LAYERS, rank, width), F32),
            pltpu.VMEM((LAYERS, owners, chunk, 2 * rank), BF16),
            pltpu.VMEM((LAYERS, owners, chunk, 2 * rank), BF16),
            pltpu.VMEM((LAYERS, chunk, 2 * rank), BF16),
            pltpu.VMEM((LAYERS, owners, chunk, 2 * rank), BF16),
            dma((5 + 3 * LAYERS, members)),
            dma((5 + 3 * LAYERS, members)),
            dma((2 * LAYERS, 3 * members)),
            dma((2 * LAYERS, 3 * members)),
            dma((2, LAYERS, owners)),
            dma((2, LAYERS, owners)),
            pltpu.VMEM((PIX + HALO, 9 * PIX), BF16),
            dma((3,)),
        ],
        compiler_params=pltpu.CompilerParams(
            collective_id=0, has_side_effects=True, vmem_limit_bytes=48 * 2**20
        ),
    )(
        features, cotangent, down_factor.transpose(0, 2, 1), up_factor.transpose(0, 2, 1), core_kernel, alive, chooser,
        jnp.asarray(border_matrix(), BF16), jnp.asarray(window_matrix(), BF16),
    )
    return out, dgrad.transpose(0, 2, 1), cgrad, ugrad.transpose(0, 2, 1)


def solution(mesh):
    return jax.shard_map(
        functools.partial(local, tuple(mesh.shape[a] for a in ("tiles", "sub", "chan"))),
        mesh=mesh,
        in_specs=(
            P(("groups", "tiles", "sub"), "chan", None),
            P(("groups", "tiles", "sub"), "chan", None),
            P(None, "chan", None),
            P(),
            P(None, "chan", None),
            P(("groups", "tiles", "sub")),
            P(("groups", "tiles", "sub"), None),
            P(("groups", "tiles", "sub"), None),
        ),
        out_specs=(
            P(("groups", "tiles", "sub"), "chan", None),
            P("groups", "chan", None),
            P("groups", None, "chan", None),
            P("groups", "chan", None),
        ),
        check_vma=False,
    )
```
